32 devices in a mesh: scene: 2 (over x), az: 8 (over z, y), rg: 2 (over core).
Axes of the slice: x: 2, y: 2, z: 4, core: 2. Of those that a mesh axis runs over, the one named last changes fastest.
Arguments:
- complex_phase_image: float32 [2, 1024, 1024], P(None, ('scene', 'az'), 'rg'), parts along dimension 1, may hold values from -6 to 6
- phase_to_topography_factor: float32 [1024, 1024], P(('scene', 'az'), 'rg'), parts along dimension 0, may hold values from 0.5 to 3
- terrain_model_heights: float32 [128, 16, 1024], P(('scene', 'az'), 'rg'), parts along dimension 0, may hold values from -6 to 6
- radar_parcel_listing: int32 [32, 9], P(('scene', 'az', 'rg')), parts along dimension 0, may hold values from -1 to 1023, as said below
- pixel_terrain_position: int32 [1024, 1024], P(('scene', 'az'), 'rg'), parts along dimension 0, may hold values from 0 to 9215, as said below
- multilook_receiving_patch: int32 [65536, 1], P(('scene', 'az', 'rg')), parts along dimension 0, may hold values from 0 to 15; in each aligned block of 2048 rows (0 to 2047, 2048 to 4095, ...) at most 256 rows name the same one
- multilook_base_point: int32 [65536], P(('scene', 'az', 'rg')), parts along dimension 0, may hold values from 0 to 2047
- multilook_splat_shares: float32 [4, 65536], P(None, ('scene', 'az', 'rg')), parts along dimension 1, may hold values from 0 to 1
Outputs:
- geocoded: float32 [2, 256, 256], P(None, ('scene', 'az'), 'rg'), parts along dimension 1
The draws below stay inside these ranges and needn't reach their ends.
There are 2 independent parts, one for each index of `scene`. The reference program is written for one: setup_inputs(seed, part) draws one part's arguments, and reference() takes and returns one part's arrays. A program takes and returns all parts, laid end to end along the dimension named above; each array names one. Nothing has to cross between parts.
Inputs may be any that keep to these rules, and one draw needn't show every extreme that they name: `radar_parcel_listing`: entries are sub-block numbers lat * 16 + lon; each tile lists a rectangle of at most 3 x 3 sub-blocks in row-major order, then -1 padding. Tile (a, r) lists only sub-blocks with c * 8 - 1 <= lat <= (c + 1) * 8 for one map latitude row c (any row, not tied to a) and r * 8 - 1 <= lon <= (r + 1) * 8. Some tile has exactly 9 listed blocks. pixel_terrain_position // 1024 is a listed, non-padding slot of the pixel's own tile. `multilook_receiving_patch`: among the rows of one device (aligned blocks of 2048 rows) at most 256 name one map tile; some map tile is named by exactly 256 rows of some device.
All inputs are finite; a program needn't handle non-finite values.
Results may differ from the reference program's by a relative error of at most 0.00015.
Values sent between devices are 32-bit elements; how exact they have to be, the bound alone decides.
A program may use at most 64 MiB of HBM per device.

```python
import math
import jax
import jax.numpy as jnp
import numpy as np
from jax import lax

AZIMUTH_PER_TILE = 64
RANGE_PER_TILE = 512
PATCH = 64
LOOK = 4
SB_A = 8
SB_R = 8
PARCEL_SAMPLES = 1024
FOOTPRINT_SLOTS = 9
TILE_COUNT = 16
ML = 16
MW = 128
LOOKS_DEV = 2048
CAP = 256
RAZ = 512
RRG = 1024
NORTHWARD_PARTS = 64
EASTWARD_PARTS = 16
MLAT = 128
MLON = 256
N_AZ = 8
N_RG = 2


def footprint_table(key):
    keys = jax.random.split(jax.random.fold_in(key, 11), 6)
    tile_ids = jnp.arange(TILE_COUNT, dtype=jnp.int32)
    tile_az = tile_ids // N_RG
    tile_rg = tile_ids % N_RG
    forced = jax.random.randint(keys[0], (), 0, TILE_COUNT)
    is_forced = tile_ids == forced
    row_shift = jax.random.randint(keys[5], (TILE_COUNT,), 0, N_AZ)
    row_shift = jnp.where(is_forced, N_AZ // 2, row_shift)
    target_az = (tile_az + row_shift) % N_AZ
    height_blocks = jnp.where(is_forced, 3, jax.random.randint(keys[1], (TILE_COUNT,), 1, 4))
    width_blocks = jnp.where(is_forced, 3, jax.random.randint(keys[2], (TILE_COUNT,), 1, 4))
    lat_low = jnp.maximum(target_az * SB_A - 1, 0)
    lat_high = jnp.minimum((target_az + 1) * SB_A, NORTHWARD_PARTS - 1) - height_blocks + 2
    lon_low = jnp.maximum(tile_rg * SB_R - 1, 0)
    lon_high = jnp.minimum((tile_rg + 1) * SB_R, EASTWARD_PARTS - 1) - width_blocks + 2
    lat_start = jax.random.randint(keys[3], (TILE_COUNT,), lat_low, lat_high)
    lon_start = jax.random.randint(keys[4], (TILE_COUNT,), lon_low, lon_high)
    lat_start = jnp.where(is_forced, jnp.minimum(target_az * SB_A, NORTHWARD_PARTS - 3), lat_start)
    lon_start = jnp.where(is_forced, jnp.minimum(tile_rg * SB_R, EASTWARD_PARTS - 3), lon_start)
    slot_ids = jnp.arange(FOOTPRINT_SLOTS, dtype=jnp.int32)[None, :]
    down_step = slot_ids // width_blocks[:, None]
    side_step = slot_ids % width_blocks[:, None]
    inside = slot_ids < (height_blocks * width_blocks)[:, None]
    numbers = (lat_start[:, None] + down_step) * EASTWARD_PARTS + lon_start[:, None] + side_step
    table_out = jnp.where(inside, numbers, -1).astype(jnp.int32)
    return (table_out, (height_blocks * width_blocks).astype(jnp.int32))


def draw_radar_parcel_listing(key, part):
    return footprint_table(key)[0]


def draw_pixel_terrain_position(key, part):
    listed = footprint_table(key)[1]
    pixel_rows = jnp.arange(RAZ, dtype=jnp.int32) // AZIMUTH_PER_TILE
    pixel_cols = jnp.arange(RRG, dtype=jnp.int32) // RANGE_PER_TILE
    pixel_tile = pixel_rows[:, None] * N_RG + pixel_cols[None, :]
    limit = listed[pixel_tile] * PARCEL_SAMPLES
    return jax.random.randint(jax.random.fold_in(key, 23), (RAZ, RRG), 0, limit).astype(jnp.int32)


def with_ends(result, rng, least, top_value):
    index_at = [jax.random.randint(jax.random.fold_in(rng, axis), (), 0, length) for axis, length in enumerate(result.shape)]
    longest = result.shape.index(max(result.shape))
    beside = index_at[:longest] + [(index_at[longest] + 1) % result.shape[longest]] + index_at[longest + 1:]
    return result.at[tuple(index_at)].set(least).at[tuple(beside)].set(top_value)


def block_scale(stream_key, dims, cuts, least, high):
    factor_of = 1.0
    for dim, shards_of in cuts:
        steps = jax.random.uniform(jax.random.fold_in(jax.random.fold_in(stream_key, 6), dim), (shards_of,), jnp.float32, least / len(cuts), high / len(cuts))
        factor_of = factor_of * jnp.repeat(jnp.exp(steps), dims[dim] // shards_of).reshape((-1,) + (1,) * (len(dims) - 1 - dim))
    return factor_of


def deal_out(stream_key, own, number, rows, count, top, most, skew):
    order = jax.random.permutation(stream_key, count)
    crowded, ordinary = load_shares(count, rows * top, most, skew, True), load_shares(count, rows * top, most, skew, False)
    places = jnp.arange(count)

    def named(sizes, turn):
        used = int((sizes > 0).sum())
        fixed = max(1, used // 4)
        moved = fixed + (places - fixed + turn * (used - fixed)) % max(1, count - fixed)
        return jnp.zeros((count,), jnp.int32).at[order[jnp.where(places < fixed, places, moved)]].set(jnp.asarray(sizes, jnp.int32))

    sizes = jnp.where(number % 4 == 0, named(crowded, number // 4), named(ordinary, number - number // 4 - 1))
    mixed = jax.random.permutation(jax.random.fold_in(own, 3), count)
    giver, sink = mixed[0:count // 2 * 2:2], mixed[1:count // 2 * 2:2]
    margin = jnp.minimum(sizes[giver] - 1, most - sizes[sink]) // 2
    margin = jnp.where((giver == order[0]) | (sink == order[0]) | (sizes[sink] == 0), 0, jnp.maximum(margin, 0))
    moved = jax.random.randint(jax.random.fold_in(own, 4), (count // 2,), 0, 1 << 20) % (margin + 1)
    sizes = sizes.at[giver].add(-moved).at[sink].add(moved)
    labels = jnp.searchsorted(jnp.cumsum(sizes), jnp.arange(rows * top), side="right").astype(jnp.int32)
    grid = labels.reshape(top, rows).T
    grid = grid[jax.random.permutation(jax.random.fold_in(own, 1), rows)]
    turn = jax.random.randint(jax.random.fold_in(own, 2), (rows, 1), 0, top)
    return jnp.take_along_axis(grid, (jnp.arange(top)[None, :] + turn) % top, axis=1)


def load_shares(count, total, bound, skew, full):
    portions = [(1 << 20) // math.isqrt(rank ** skew) + 1 for rank in range(1, count + 1)]
    largest = bound if full else min(bound, max(-(-total // count), total * portions[0] // sum(portions)))
    least = 1 if total - largest >= count - 1 else 0
    given, surplus = [largest] + [least] * (count - 1), total - largest - least * (count - 1)
    while surplus > 0:
        candidates = [i for i in range(1, count) if given[i] < largest] or [i for i in range(1, count) if given[i] < bound]
        whole, budget = sum([portions[i] for i in candidates]), surplus
        for i in candidates:
            extra = min(bound - given[i], max(1, budget * portions[i] // whole), surplus)
            given[i] = given[i] + extra
            surplus = surplus - extra
    return np.array(given)


def centred(own_key, extent, deviation, reach, cuts=(), held_as=jnp.bfloat16):
    level = block_scale(own_key, extent, cuts, -0.22, 0.18) if cuts else 1.0
    values = jax.random.normal(own_key, extent, jnp.float32) * deviation * level
    return jnp.minimum(jnp.maximum(values, -reach), reach).astype(held_as)


def setup_inputs(seed: int = 0, part: int = 0) -> dict:
    splits = jax.random.split(jax.random.key(seed), 9)
    part_keys = jax.random.split(jax.random.fold_in(splits[8], part), 9)
    complex_phase_image = centred(part_keys[0], (2, RAZ, RRG), 1.0, 6.0, ((1, 8), (2, 2)), jnp.float32)
    phase_to_topography_factor = jnp.clip(0.5 + 2.5 * jax.random.uniform(part_keys[1], (RAZ, RRG), jnp.float32) ** block_scale(part_keys[1], (RAZ, RRG), ((0, 8), (1, 2)), -0.2, 0.2), 0.5, 3.0)
    terrain_model_heights = centred(part_keys[2], (NORTHWARD_PARTS, EASTWARD_PARTS, PARCEL_SAMPLES), 1.0, 6.0, ((0, 8), (1, 2)), jnp.float32)
    radar_parcel_listing = draw_radar_parcel_listing(jax.random.fold_in(jax.random.fold_in(splits[8], part), 71), part)
    pixel_terrain_position = draw_pixel_terrain_position(jax.random.fold_in(jax.random.fold_in(splits[8], part), 71), part)
    multilook_receiving_patch_keys = jax.random.split(jax.random.fold_in(part_keys[5], 1), (TILE_COUNT * LOOKS_DEV) // LOOKS_DEV)
    multilook_receiving_patch_turns = jax.random.permutation(jax.random.fold_in(part_keys[5], 3), (TILE_COUNT * LOOKS_DEV) // LOOKS_DEV)
    multilook_receiving_patch = jax.vmap(lambda own, number: deal_out(jax.random.fold_in(part_keys[5], 2), own, number, LOOKS_DEV, TILE_COUNT, 1, CAP, 2))(multilook_receiving_patch_keys, multilook_receiving_patch_turns).reshape((TILE_COUNT * LOOKS_DEV, 1))
    multilook_base_point = with_ends(jax.random.randint(part_keys[6], (TILE_COUNT * LOOKS_DEV,), 0, ML * MW), jax.random.fold_in(part_keys[6], 1), 0, (ML * MW) - 1).astype(jnp.int32)
    multilook_splat_shares = jnp.clip(1.0 * jax.random.uniform(part_keys[7], (4, TILE_COUNT * LOOKS_DEV), jnp.float32) ** block_scale(part_keys[7], (4, TILE_COUNT * LOOKS_DEV), ((1, 16),), -0.2, 0.2), 0.0, 1.0)
    return {"complex_phase_image": complex_phase_image, "phase_to_topography_factor": phase_to_topography_factor, "terrain_model_heights": terrain_model_heights, "radar_parcel_listing": radar_parcel_listing, "pixel_terrain_position": pixel_terrain_position, "multilook_receiving_patch": multilook_receiving_patch, "multilook_base_point": multilook_base_point, "multilook_splat_shares": multilook_splat_shares}


EPS = 1e-06

def box_mean(magnitude):
    summed = jnp.zeros_like(magnitude)
    for shift_a in (-1, 0, 1):
        for shift_b in (-1, 0, 1):
            summed = summed + jnp.roll(jnp.roll(magnitude, shift_a, axis=1), shift_b, axis=2)
    return summed / 9.0

def reference(complex_phase_image, phase_to_topography_factor, terrain_model_heights, radar_parcel_listing, pixel_terrain_position, multilook_receiving_patch, multilook_base_point, multilook_splat_shares):
    terrain_raveled = terrain_model_heights.reshape(NORTHWARD_PARTS * EASTWARD_PARTS, PARCEL_SAMPLES)
    block_grid = terrain_raveled[jnp.maximum(radar_parcel_listing, 0)].reshape(TILE_COUNT, FOOTPRINT_SLOTS * PARCEL_SAMPLES)
    index_of_tile = pixel_terrain_position.reshape(N_AZ, AZIMUTH_PER_TILE, N_RG, RANGE_PER_TILE).transpose(0, 2, 1, 3).reshape(TILE_COUNT, AZIMUTH_PER_TILE * RANGE_PER_TILE)
    height_values = jnp.take_along_axis(block_grid, index_of_tile, axis=1)
    height_values = height_values.reshape(N_AZ, N_RG, AZIMUTH_PER_TILE, RANGE_PER_TILE).transpose(0, 2, 1, 3).reshape(RAZ, RRG)
    topo_phase = phase_to_topography_factor * height_values
    cosine_phase = jnp.cos(topo_phase)
    sine_phase = jnp.sin(topo_phase)
    real_part = complex_phase_image[0] * cosine_phase + complex_phase_image[1] * sine_phase
    imag_part = complex_phase_image[1] * cosine_phase - complex_phase_image[0] * sine_phase
    rim = PATCH // 4
    step = PATCH // 2
    padded = jnp.pad(jnp.stack([real_part, imag_part]), ((0, 0), (rim, rim), (rim, rim)))
    block_cols = RRG // step

    def filter_row(strip_index):
        strip = lax.dynamic_slice_in_dim(padded, strip_index * step, PATCH, axis=1)
        pieces = strip.reshape(2, PATCH, block_cols + 1, step)
        pairs = jnp.concatenate([pieces[:, :, :-1], pieces[:, :, 1:]], axis=3)
        complex_field = (pairs[0] + 1j * pairs[1]).transpose(1, 0, 2)
        spectrum = jnp.fft.fft2(complex_field)
        smooth = box_mean(jnp.abs(spectrum))
        spectral_gain = jnp.sqrt(smooth / (lax.optimization_barrier(jnp.mean(smooth, axis=(1, 2), keepdims=True)) + EPS))
        restored = jnp.fft.ifft2(spectrum * spectral_gain)[:, rim:rim + step, rim:rim + step]
        core_cells = restored.transpose(1, 0, 2).reshape(step, block_cols * step)
        return jnp.stack([jnp.real(core_cells), jnp.imag(core_cells)])
    strips = lax.map(filter_row, jnp.arange(RAZ // step, dtype=jnp.int32))
    filtered = strips.transpose(1, 0, 2, 3).reshape(2, RAZ, RRG)
    looks = filtered.reshape(2, RAZ // LOOK, LOOK, RRG // LOOK, LOOK).mean(axis=(2, 4))
    looks = looks.reshape(2, N_AZ, ML, N_RG, MW).transpose(0, 1, 3, 2, 4).reshape(2, TILE_COUNT * LOOKS_DEV)
    owner_tile = multilook_receiving_patch[:, 0]
    lat_cell = owner_tile // N_RG * ML + multilook_base_point // MW
    lon_cell = owner_tile % N_RG * MW + multilook_base_point % MW
    stride = MLON + 1
    base = lat_cell * stride + lon_cell
    corners = jnp.concatenate([base, base + 1, base + stride, base + stride + 1])
    weights = multilook_splat_shares.reshape(-1)
    contributions = jnp.stack([jnp.tile(looks[0], 4) * weights, jnp.tile(looks[1], 4) * weights, weights])
    accumulated = jnp.zeros((3, (MLAT + 1) * stride), dtype=jnp.float32).at[:, corners].add(contributions)
    grid_sums = accumulated.reshape(3, MLAT + 1, stride)[:, :MLAT, :MLON]
    return grid_sums[:2] / jnp.maximum(grid_sums[2:3], 1.0)
```

```python
import functools
import math

import jax
import jax.numpy as jnp
import numpy as np
from jax import lax
from jax.experimental import pallas as pl
from jax.experimental.pallas import tpu as pltpu
from jax.sharding import PartitionSpec as P

PATCH = 64
LOOK = 4
LANES = 128
EPS = 1e-06
F32 = jnp.float32
BF16 = jnp.bfloat16


def padded_2(value, sides, width):
    for axis, dim in sides:
        size, length = (lax.axis_size(axis), value.shape[dim])
        up = [(i, (i + 1) % size) for i in range(size - 1)]
        down = [(j, i) for i, j in up]
        last = lax.slice_in_dim(value, length - width, length, axis=dim)
        first = lax.slice_in_dim(value, 0, width, axis=dim)
        before = lax.ppermute(last, axis, up)
        after = lax.ppermute(first, axis, down)
        value = jnp.concatenate([before, value, after], axis=dim)
    return value


def block_coords(block_lists, nlon_count):
    clipped = jnp.maximum(block_lists, 0)
    return (clipped // nlon_count, clipped % nlon_count)


def entry_rank(owner_key, is_valid):
    slots = owner_key.shape[-1]
    same_owner = (owner_key[:, :, None] == owner_key[:, None, :]) & is_valid[:, None, :]
    slot_ids = jnp.arange(slots, dtype=jnp.int32)
    earlier = slot_ids[None, :] < slot_ids[:, None]
    return jnp.sum((same_owner & earlier[None]).astype(jnp.int32), axis=2)


def pack_blocks(block_lists, owner_key, local_block, source_rows, self_key):
    slots = block_lists.shape[-1]
    is_valid = block_lists >= 0
    rank_within = entry_rank(owner_key, is_valid)
    slot_ids = jnp.arange(slots, dtype=jnp.int32)
    matches = (is_valid & (owner_key == self_key))[:, :, None] & (
        rank_within[:, :, None] == slot_ids[None, None, :]
    )
    picked = jnp.sum(jnp.where(matches, local_block[:, :, None], 0), axis=1)
    present = jnp.any(matches, axis=1)
    return jnp.where(present[..., None], source_rows[picked], 0.0)


def unpack_blocks(own_list, owner_key, received):
    slots = own_list.shape[-1]
    is_valid = own_list >= 0
    rank_within = entry_rank(owner_key[None], is_valid[None])[0]
    position = jnp.where(is_valid, owner_key * slots + rank_within, 0)
    return received.reshape(-1, received.shape[-1])[position]


def halves(value):
    high = value.astype(BF16)
    return high, (value - high.astype(F32)).astype(BF16)


def dot3(left, right):
    left_high, left_low = left
    right_high, right_low = right
    out = jnp.dot(left_high, right_high, preferred_element_type=F32)
    out = out + jnp.dot(left_low, right_high, preferred_element_type=F32)
    return out + jnp.dot(left_high, right_low, preferred_element_type=F32)


def filter_tables():
    steps = np.arange(PATCH)
    angle = (steps[:, None] * steps[None, :] % PATCH) * (2.0 * math.pi / PATCH)
    cosine, sine = np.cos(angle), np.sin(angle)
    left = np.block([[cosine, sine], [-sine, cosine]])
    step, wide = PATCH // 2, 4 * PATCH
    right = np.zeros((2 * wide, 2 * wide))
    for p in range(4):
        rows, cols = slice(p * step, p * step + PATCH), slice(p * PATCH, (p + 1) * PATCH)
        rows_im = slice(wide + p * step, wide + p * step + PATCH)
        cols_im = slice(wide + p * PATCH, wide + (p + 1) * PATCH)
        right[rows, cols] = cosine
        right[rows, cols_im] = -sine
        right[rows_im, cols] = sine
        right[rows_im, cols_im] = cosine
    group = np.arange(wide) // PATCH
    same = group[:, None] == group[None, :]
    gap = (np.arange(wide)[:, None] - np.arange(wide)[None, :]) % PATCH
    band = same & ((gap <= 1) | (gap == PATCH - 1))
    cells = PATCH // 2 // LOOK
    places = PATCH // 4 + np.arange(cells * LOOK)
    turn = steps[:, None] * places[None, :] % PATCH * (2.0 * math.pi / PATCH)
    mean_re = np.cos(turn).reshape(PATCH, cells, LOOK).mean(axis=2) / PATCH
    mean_im = np.sin(turn).reshape(PATCH, cells, LOOK).mean(axis=2) / PATCH
    back_left = np.block([[mean_re.T, -mean_im.T], [mean_im.T, mean_re.T]])
    back_right = np.zeros((2 * wide, 8 * cells))
    for p in range(4):
        rows = slice(p * PATCH, (p + 1) * PATCH)
        rows_im = slice(wide + p * PATCH, wide + (p + 1) * PATCH)
        cols = slice(p * cells, (p + 1) * cells)
        cols_im = slice((4 + p) * cells, (5 + p) * cells)
        back_right[rows, cols] = mean_re
        back_right[rows, cols_im] = mean_im
        back_right[rows_im, cols] = -mean_im
        back_right[rows_im, cols_im] = mean_re
    tables = []
    for table in (left, right, back_left, back_right):
        high = table.astype(np.float32).astype(jnp.bfloat16)
        tables += [high, (table - high.astype(np.float64)).astype(jnp.bfloat16)]
    return tables + [band.astype(jnp.bfloat16), same.astype(jnp.bfloat16)]


def sine_cosine(angle):
    turns = jnp.floor(angle * (2.0 / math.pi) + 0.5)
    rest = angle - turns * 1.5703125
    rest = rest - turns * 4.837512969970703e-04
    rest = rest - turns * 7.549789948768648e-08
    square = rest * rest
    sine = ((-1.9515295891e-4 * square + 8.3321608736e-3) * square - 1.6666654611e-1) * square
    sine = sine * rest + rest
    cosine = ((2.443315711809948e-5 * square - 1.388731625493765e-3) * square + 4.166664568298827e-2)
    cosine = cosine * square * square - 0.5 * square + 1.0
    quarter = turns.astype(jnp.int32) & 3
    swap = (quarter & 1) == 1
    sine_out = jnp.where(swap, cosine, sine)
    cosine_out = jnp.where(swap, sine, cosine)
    sine_out = jnp.where(quarter >= 2, -sine_out, sine_out)
    cosine_out = jnp.where((quarter == 1) | (quarter == 2), -cosine_out, cosine_out)
    return sine_out, cosine_out


def flatten_tile(image_ref, factor_ref, position_ref, table_ref, flat_ref):
    lines, samples = factor_ref.shape
    slots, parcel = table_ref.shape
    for column in range(samples // LANES):
        span = slice(column * LANES, (column + 1) * LANES)
        position = position_ref[:, span]
        lane = position & (LANES - 1)
        row = lax.shift_right_logical(position, LANES.bit_length() - 1)

        heights = jnp.zeros((lines, LANES), F32)
        for slot in range(slots):
            for part in range(parcel // LANES):
                source = table_ref[slot : slot + 1, part * LANES : (part + 1) * LANES]
                picked = jnp.take_along_axis(
                    jnp.broadcast_to(source, (lines, LANES)), lane, axis=1
                )
                heights = jnp.where(row == slot * (parcel // LANES) + part, picked, heights)
        sine, cosine = sine_cosine(factor_ref[:, span] * heights)
        real, imag = image_ref[0, :, span], image_ref[1, :, span]
        flat_ref[0, :, span] = real * cosine + imag * sine
        flat_ref[1, :, span] = imag * cosine - real * sine


def goldstein_looks(padded, tables):
    left = (tables[0][...], tables[1][...])
    right = (tables[2], tables[3])
    back_left = (tables[4][...], tables[5][...])
    back_right = (tables[6], tables[7])
    band, same = tables[8][...], tables[9][...]
    step, wide = PATCH // 2, 4 * PATCH
    lines, samples = padded.shape[1:]
    block_rows = (lines - step) // step
    groups = (samples - LANES) // LANES
    columns = []
    for u in range(block_rows):
        strip = jnp.concatenate(
            [padded[0, u * step : u * step + PATCH], padded[1, u * step : u * step + PATCH]], axis=0
        )
        columns.append(dot3(left, halves(strip)))
    real = halves(jnp.concatenate([c[:PATCH] for c in columns], axis=0))
    imag = halves(jnp.concatenate([c[PATCH:] for c in columns], axis=0))
    rows_re, rows_im = [], []
    for q in range(groups):
        window = slice(q * LANES, q * LANES + wide)
        spectrum = dot3(
            (real[0][:, window], real[1][:, window]), (right[0][:wide], right[1][:wide])
        ) + dot3((imag[0][:, window], imag[1][:, window]), (right[0][wide:], right[1][wide:]))
        spec_re, spec_im = spectrum[:, :wide], spectrum[:, wide:]
        size = jnp.sqrt(spec_re * spec_re + spec_im * spec_im)
        size_high, size_low = halves(size)
        across = jnp.dot(size_high, band, preferred_element_type=F32) + jnp.dot(
            size_low, band, preferred_element_type=F32
        )
        gains = []
        for u in range(block_rows):
            part = across[u * PATCH : (u + 1) * PATCH]
            around = part + pltpu.roll(part, 1, 0) + pltpu.roll(part, PATCH - 1, 0)
            column = jnp.sum(size[u * PATCH : (u + 1) * PATCH], axis=0, keepdims=True)
            column_high, column_low = halves(jnp.broadcast_to(column, (16, wide)))
            total = jnp.dot(column_high, same, preferred_element_type=F32) + jnp.dot(
                column_low, same, preferred_element_type=F32
            )
            scale = (1.0 / 9.0) / (total[:1] * (1.0 / PATCH**2) + EPS)
            gains.append(jnp.sqrt(around * scale))
        gain = jnp.concatenate(gains, axis=0)
        rows = dot3(halves(spec_re * gain), (back_right[0][:wide], back_right[1][:wide])) + dot3(
            halves(spec_im * gain), (back_right[0][wide:], back_right[1][wide:])
        )
        half = rows.shape[1] // 2
        rows_re.append(rows[:, :half])
        rows_im.append(rows[:, half:])
    rows_re = jnp.concatenate(rows_re, axis=1)
    rows_im = jnp.concatenate(rows_im, axis=1)
    looks = []
    for u in range(block_rows):
        rows = slice(u * PATCH, (u + 1) * PATCH)
        looks.append(dot3(back_left, halves(jnp.concatenate([rows_re[rows], rows_im[rows]], axis=0))))
    half = looks[0].shape[0] // 2
    return [jnp.concatenate([x[:half] for x in looks], axis=0), jnp.concatenate([x[half:] for x in looks], axis=0)]


def place_looks(owner_ref, base_ref, share_ref, row_ref, hit_ref, map_lat, map_lon, tile_lat, tile_lon):
    chunks = owner_ref.shape[0]
    count_rg = map_lon // tile_lon
    owner, base = owner_ref[...], base_ref[...]
    anchor_row = owner // count_rg * tile_lat + base // tile_lon
    anchor_col = owner % count_rg * tile_lon + base % tile_lon
    row_ids = lax.broadcasted_iota(jnp.int32, (map_lat, LANES), 0)
    col_ids = lax.broadcasted_iota(jnp.int32, (map_lon, LANES), 0)
    for i in range(chunks):
        span = slice(i * LANES, (i + 1) * LANES)
        hit_ref[:, span] = (col_ids == anchor_col[i : i + 1]).astype(F32).astype(BF16)
        gap = row_ids - anchor_row[i : i + 1]
        for c in range(2):
            upper, lower = share_ref[c, i : i + 1, :], share_ref[2 + c, i : i + 1, :]
            row_ref[c, :, span] = jnp.where(gap == 0, upper, jnp.where(gap == 1, lower, 0.0))


def splat(row_ref, hit_ref, look):
    dims = (((1,), (1,)), ((), ()))
    chunks = hit_ref.shape[1] // LANES
    sums = []
    for c in range(2):
        if look is None:
            value = row_ref[c]
        else:
            value = jnp.concatenate(
                [row_ref[c, :, i * LANES : (i + 1) * LANES] * look[i : i + 1] for i in range(chunks)],
                axis=1,
            )
        high, low = halves(value)
        sums.append(
            lax.dot_general(high, hit_ref[...], dims, preferred_element_type=F32)
            + lax.dot_general(low, hit_ref[...], dims, preferred_element_type=F32)
        )
    moved = pltpu.roll(sums[1], 1, 1)
    first = lax.broadcasted_iota(jnp.int32, moved.shape, 1) == 0
    return sums[0] + jnp.where(first, 0.0, moved)


def filter_kernel(tile_shape, padded_ref, owner_ref, base_ref, share_ref, *refs):
    tables, (out_ref, row_ref, hit_ref) = refs[:10], refs[10:]
    map_lat, map_lon = out_ref.shape[1:]
    place_looks(owner_ref, base_ref, share_ref, row_ref, hit_ref, map_lat, map_lon, *tile_shape)
    looks = goldstein_looks(padded_ref, tables)
    out_ref[0] = splat(row_ref, hit_ref, looks[0])
    out_ref[1] = splat(row_ref, hit_ref, looks[1])
    out_ref[2] = splat(row_ref, hit_ref, None)


def body(
    complex_phase_image,
    phase_to_topography_factor,
    terrain_model_heights,
    radar_parcel_listing,
    pixel_terrain_position,
    multilook_receiving_patch,
    multilook_base_point,
    multilook_splat_shares,
):
    count_az = lax.axis_size("az")
    count_rg = lax.axis_size("rg")
    self_az = lax.axis_index("az")
    self_rg = lax.axis_index("rg")
    parcel_north_coordinate, parcel_east_coordinate, number_terrain_points = (
        terrain_model_heights.shape
    )
    nlon_count = parcel_east_coordinate * count_rg
    own_list = radar_parcel_listing[0]
    lat_own, lon_own = block_coords(own_list, nlon_count)
    all_lists = lax.all_gather(radar_parcel_listing, ("az", "rg"), axis=0, tiled=True)
    lat_all, lon_all = block_coords(all_lists, nlon_count)
    key_all = lat_all // parcel_north_coordinate * count_rg + lon_all // parcel_east_coordinate
    local_all = (lat_all - self_az * parcel_north_coordinate) * parcel_east_coordinate + (
        lon_all - self_rg * parcel_east_coordinate
    )
    outgoing = pack_blocks(
        all_lists,
        key_all,
        local_all,
        terrain_model_heights.reshape(
            parcel_north_coordinate * parcel_east_coordinate, number_terrain_points
        ),
        self_az * count_rg + self_rg,
    )
    received = lax.all_to_all(outgoing, ("az", "rg"), split_axis=0, concat_axis=0, tiled=True)
    key_own = lat_own // parcel_north_coordinate * count_rg + lon_own // parcel_east_coordinate
    height_lookup_table = unpack_blocks(own_list, key_own, received)
    az_lines, rg_samples = phase_to_topography_factor.shape
    flattened = pl.pallas_call(
        flatten_tile,
        out_shape=jax.ShapeDtypeStruct((2, az_lines, rg_samples), F32),
        name="flatten",
    )(complex_phase_image, phase_to_topography_factor, pixel_terrain_position, height_lookup_table)
    rim = PATCH // 4
    padded = padded_2(flattened, (("az", 1), ("rg", 2)), rim)
    padded = jnp.pad(padded, ((0, 0), (0, 0), (0, LANES - 2 * rim)))
    map_lat = az_lines // LOOK
    map_lon = rg_samples // LOOK
    chunks = map_lat * map_lon // LANES
    tables = filter_tables()
    sums = pl.pallas_call(
        functools.partial(filter_kernel, (map_lat, map_lon)),
        out_shape=jax.ShapeDtypeStruct((3, map_lat * count_az, map_lon * count_rg), F32),
        scratch_shapes=[
            pltpu.VMEM((2, map_lat * count_az, chunks * LANES), F32),
            pltpu.VMEM((map_lon * count_rg, chunks * LANES), BF16),
        ],
        compiler_params=pltpu.CompilerParams(vmem_limit_bytes=48 * 1024 * 1024),
        name="filter_splat",
    )(
        padded,
        multilook_receiving_patch.reshape(chunks, LANES),
        multilook_base_point.reshape(chunks, LANES),
        multilook_splat_shares.reshape(4, chunks, LANES),
        *tables,
    )
    sums = lax.psum_scatter(sums, "rg", scatter_dimension=2, tiled=True)
    sums = lax.psum_scatter(sums, "az", scatter_dimension=1, tiled=True)
    return sums[:2] / jnp.maximum(sums[2:3], 1.0)


def solution(mesh):
    return jax.shard_map(
        body,
        mesh=mesh,
        in_specs=(
            P(None, ("scene", "az"), "rg"),
            P(("scene", "az"), "rg"),
            P(("scene", "az"), "rg", None),
            P(("scene", "az", "rg"), None),
            P(("scene", "az"), "rg"),
            P(("scene", "az", "rg"), None),
            P(("scene", "az", "rg")),
            P(None, ("scene", "az", "rg")),
        ),
        out_specs=P(None, ("scene", "az"), "rg"),
        check_vma=False,
    )
```

```python
import functools
import math

import jax
import jax.numpy as jnp
import numpy as np
from jax import lax
from jax.experimental import pallas as pl
from jax.experimental.pallas import tpu as pltpu
from jax.sharding import PartitionSpec as P

PATCH = 64
LOOK = 4
LANES = 128
EPS = 1e-06
F32 = jnp.float32
BF16 = jnp.bfloat16


def halves(value):
    high = value.astype(BF16)
    return high, (value - high.astype(F32)).astype(BF16)


def dot3(left, right):
    left_high, left_low = left
    right_high, right_low = right
    out = jnp.dot(left_high, right_high, preferred_element_type=F32)
    out = out + jnp.dot(left_low, right_high, preferred_element_type=F32)
    return out + jnp.dot(left_high, right_low, preferred_element_type=F32)


def filter_tables():
    steps = np.arange(PATCH)
    angle = (steps[:, None] * steps[None, :] % PATCH) * (2.0 * math.pi / PATCH)
    cosine, sine = np.cos(angle), np.sin(angle)
    left = np.block([[cosine, sine], [-sine, cosine]])
    step, wide = PATCH // 2, 4 * PATCH
    right = np.zeros((2 * wide, 2 * wide))
    for p in range(4):
        rows, cols = slice(p * step, p * step + PATCH), slice(p * PATCH, (p + 1) * PATCH)
        rows_im = slice(wide + p * step, wide + p * step + PATCH)
        cols_im = slice(wide + p * PATCH, wide + (p + 1) * PATCH)
        right[rows, cols] = cosine
        right[rows, cols_im] = -sine
        right[rows_im, cols] = sine
        right[rows_im, cols_im] = cosine
    group = np.arange(wide) // PATCH
    same = group[:, None] == group[None, :]
    gap = (np.arange(wide)[:, None] - np.arange(wide)[None, :]) % PATCH
    band = same & ((gap <= 1) | (gap == PATCH - 1))
    cells = PATCH // 2 // LOOK
    places = PATCH // 4 + np.arange(cells * LOOK)
    turn = steps[:, None] * places[None, :] % PATCH * (2.0 * math.pi / PATCH)
    mean_re = np.cos(turn).reshape(PATCH, cells, LOOK).mean(axis=2) / PATCH
    mean_im = np.sin(turn).reshape(PATCH, cells, LOOK).mean(axis=2) / PATCH
    back_left = np.block([[mean_re.T, -mean_im.T], [mean_im.T, mean_re.T]])
    back_right = np.zeros((2 * wide, 8 * cells))
    for p in range(4):
        rows = slice(p * PATCH, (p + 1) * PATCH)
        rows_im = slice(wide + p * PATCH, wide + (p + 1) * PATCH)
        cols = slice(p * cells, (p + 1) * cells)
        cols_im = slice((4 + p) * cells, (5 + p) * cells)
        back_right[rows, cols] = mean_re
        back_right[rows, cols_im] = mean_im
        back_right[rows_im, cols] = -mean_im
        back_right[rows_im, cols_im] = mean_re
    tables = []
    for table in (left, right, back_left, back_right):
        high = table.astype(np.float32).astype(jnp.bfloat16)
        tables += [high, (table - high.astype(np.float64)).astype(jnp.bfloat16)]
    return tables + [band.astype(jnp.bfloat16), same.astype(jnp.bfloat16)]


def sine_cosine(angle):
    turns = jnp.floor(angle * (2.0 / math.pi) + 0.5)
    rest = angle - turns * 1.5703125
    rest = rest - turns * 4.837512969970703e-04
    rest = rest - turns * 7.549789948768648e-08
    square = rest * rest
    sine = ((-1.9515295891e-4 * square + 8.3321608736e-3) * square - 1.6666654611e-1) * square
    sine = sine * rest + rest
    cosine = ((2.443315711809948e-5 * square - 1.388731625493765e-3) * square + 4.166664568298827e-2)
    cosine = cosine * square * square - 0.5 * square + 1.0
    quarter = turns.astype(jnp.int32) & 3
    swap = (quarter & 1) == 1
    sine_out = jnp.where(swap, cosine, sine)
    cosine_out = jnp.where(swap, sine, cosine)
    sine_out = jnp.where(quarter >= 2, -sine_out, sine_out)
    cosine_out = jnp.where((quarter == 1) | (quarter == 2), -cosine_out, cosine_out)
    return sine_out, cosine_out


def flatten_tile(image_ref, factor_ref, position_ref, table_ref, flat_ref):
    lines, samples = factor_ref.shape
    rows = table_ref.shape[0]
    for column in range(samples // LANES):
        span = slice(column * LANES, (column + 1) * LANES)
        position = position_ref[:, span]
        lane = position & (LANES - 1)
        row = lax.shift_right_logical(position, LANES.bit_length() - 1)

        heights = jnp.zeros((lines, LANES), F32)
        for r in range(rows):
            picked = jnp.take_along_axis(
                jnp.broadcast_to(table_ref[r : r + 1], (lines, LANES)), lane, axis=1, mode="promise_in_bounds"
            )
            heights = jnp.where(row == r, picked, heights)
        sine, cosine = sine_cosine(factor_ref[:, span] * heights)
        real, imag = image_ref[0, :, span], image_ref[1, :, span]
        flat_ref[0, :, span] = real * cosine + imag * sine
        flat_ref[1, :, span] = imag * cosine - real * sine


def goldstein_looks(padded, tables):
    left = (tables[0][...], tables[1][...])
    right = (tables[2], tables[3])
    back_left = (tables[4][...], tables[5][...])
    back_right = (tables[6], tables[7])
    band, same = tables[8][...], tables[9][...]
    step, wide = PATCH // 2, 4 * PATCH
    lines, samples = padded.shape[1:]
    block_rows = (lines - step) // step
    groups = (samples - LANES) // LANES
    columns = []
    for u in range(block_rows):
        strip = jnp.concatenate(
            [padded[0, u * step : u * step + PATCH], padded[1, u * step : u * step + PATCH]], axis=0
        )
        columns.append(dot3(left, halves(strip)))
    real = halves(jnp.concatenate([c[:PATCH] for c in columns], axis=0))
    imag = halves(jnp.concatenate([c[PATCH:] for c in columns], axis=0))
    rows_re, rows_im = [], []
    for q in range(groups):
        window = slice(q * LANES, q * LANES + wide)
        spectrum = dot3(
            (real[0][:, window], real[1][:, window]), (right[0][:wide], right[1][:wide])
        ) + dot3((imag[0][:, window], imag[1][:, window]), (right[0][wide:], right[1][wide:]))
        spec_re, spec_im = spectrum[:, :wide], spectrum[:, wide:]
        size = jnp.sqrt(spec_re * spec_re + spec_im * spec_im)
        size_high, size_low = halves(size)
        across = jnp.dot(size_high, band, preferred_element_type=F32) + jnp.dot(
            size_low, band, preferred_element_type=F32
        )
        gains = []
        for u in range(block_rows):
            part = across[u * PATCH : (u + 1) * PATCH]
            around = part + pltpu.roll(part, 1, 0) + pltpu.roll(part, PATCH - 1, 0)
            column = jnp.sum(size[u * PATCH : (u + 1) * PATCH], axis=0, keepdims=True)
            column_high, column_low = halves(jnp.broadcast_to(column, (16, wide)))
            total = jnp.dot(column_high, same, preferred_element_type=F32) + jnp.dot(
                column_low, same, preferred_element_type=F32
            )
            scale = (1.0 / 9.0) / (total[:1] * (1.0 / PATCH**2) + EPS)
            gains.append(jnp.sqrt(around * scale))
        gain = jnp.concatenate(gains, axis=0)
        rows = dot3(halves(spec_re * gain), (back_right[0][:wide], back_right[1][:wide])) + dot3(
            halves(spec_im * gain), (back_right[0][wide:], back_right[1][wide:])
        )
        half = rows.shape[1] // 2
        rows_re.append(rows[:, :half])
        rows_im.append(rows[:, half:])
    rows_re = jnp.concatenate(rows_re, axis=1)
    rows_im = jnp.concatenate(rows_im, axis=1)
    looks = []
    for u in range(block_rows):
        rows = slice(u * PATCH, (u + 1) * PATCH)
        looks.append(dot3(back_left, halves(jnp.concatenate([rows_re[rows], rows_im[rows]], axis=0))))
    half = looks[0].shape[0] // 2
    return [jnp.concatenate([x[:half] for x in looks], axis=0), jnp.concatenate([x[half:] for x in looks], axis=0)]


def place_looks(owner_ref, base_ref, share_ref, row_ref, hit_ref, map_lat, map_lon, tile_lat, tile_lon):
    chunks = owner_ref.shape[0]
    count_rg = map_lon // tile_lon
    owner, base = owner_ref[...], base_ref[...]
    anchor_row = owner // count_rg * tile_lat + base // tile_lon
    anchor_col = owner % count_rg * tile_lon + base % tile_lon
    row_ids = lax.broadcasted_iota(jnp.int32, (map_lat, LANES), 0)
    col_ids = lax.broadcasted_iota(jnp.int32, (map_lon, LANES), 0)
    for i in range(chunks):
        span = slice(i * LANES, (i + 1) * LANES)
        hit_ref[:, span] = (col_ids == anchor_col[i : i + 1]).astype(F32).astype(BF16)
        gap = row_ids - anchor_row[i : i + 1]
        for c in range(2):
            upper, lower = share_ref[c, i : i + 1, :], share_ref[2 + c, i : i + 1, :]
            row_ref[c, :, span] = jnp.where(gap == 0, upper, jnp.where(gap == 1, lower, 0.0))


def splat(row_ref, hit_ref, look):
    dims = (((1,), (1,)), ((), ()))
    chunks = hit_ref.shape[1] // LANES
    sums = []
    for c in range(2):
        if look is None:
            value = row_ref[c]
        else:
            value = jnp.concatenate(
                [row_ref[c, :, i * LANES : (i + 1) * LANES] * look[i : i + 1] for i in range(chunks)],
                axis=1,
            )
        high, low = halves(value)
        sums.append(
            lax.dot_general(high, hit_ref[...], dims, preferred_element_type=F32)
            + lax.dot_general(low, hit_ref[...], dims, preferred_element_type=F32)
        )
    moved = pltpu.roll(sums[1], 1, 1)
    first = lax.broadcasted_iota(jnp.int32, moved.shape, 1) == 0
    return sums[0] + jnp.where(first, 0.0, moved)


def filter_kernel(tile_shape, padded_ref, owner_ref, base_ref, share_ref, *refs):
    tables, (out_ref, row_ref, hit_ref) = refs[:10], refs[10:]
    map_lat, map_lon = out_ref.shape[1:]
    place_looks(owner_ref, base_ref, share_ref, row_ref, hit_ref, map_lat, map_lon, *tile_shape)
    looks = goldstein_looks(padded_ref, tables)
    out_ref[0] = splat(row_ref, hit_ref, looks[0])
    out_ref[1] = splat(row_ref, hit_ref, looks[1])
    out_ref[2] = splat(row_ref, hit_ref, None)


MESH = pl.DeviceIdType.MESH


def peers(count_az):
    az, rg = lax.axis_index("az"), lax.axis_index("rg")
    others = [{"az": lax.rem(az + d, count_az), "rg": rg} for d in range(1, count_az)]
    return az, rg, others, {"az": az, "rg": 1 - rg}


def greet(devices):
    barrier = pltpu.get_barrier_semaphore()
    for device in devices:
        pl.semaphore_signal(barrier, inc=1, device_id=device, device_id_type=MESH)
    pl.semaphore_wait(barrier, len(devices))


def remote(source, target, send_sem, recv_sem, device):
    return pltpu.make_async_remote_copy(
        src_ref=source,
        dst_ref=target,
        send_sem=send_sem,
        recv_sem=recv_sem,
        device_id=device,
        device_id_type=MESH,
    )


def terrain_kernel(
    count_az,
    parcel_shape,
    list_ref,
    terrain_ref,
    table_ref,
    extended,
    edge,
    lists,
    lists_smem,
    outgoing,
    incoming,
    edge_sems,
    list_send,
    list_recv,
    block_send,
    block_recv,
    local_sem,
):
    north, east = parcel_shape
    slots = table_ref.shape[0]
    az, rg, others, partner = peers(count_az)
    greet(others + [partner])
    list_copies = [
        remote(list_ref, lists.at[d + 1], list_send.at[d], list_recv.at[d], device)
        for d, device in enumerate(others)
    ]
    for copy in list_copies:
        copy.start()
    for lat in range(north):
        edge[lat] = jnp.where(rg == 0, terrain_ref[lat * east + east - 1], terrain_ref[lat * east])
    edge_copy = remote(
        edge, extended.at[pl.ds(north * east, north)], edge_sems.at[0], edge_sems.at[1], partner
    )
    edge_copy.start()
    extended[: north * east] = terrain_ref[...]
    extended[north * east + north] = jnp.zeros(extended.shape[1:], F32)
    lists[0] = list_ref[...]
    for copy in list_copies:
        copy.wait()
    to_smem = pltpu.make_async_copy(lists, lists_smem, local_sem)
    to_smem.start()
    edge_copy.wait()
    to_smem.wait()

    def pick(d, slot):
        number = lists_smem[d, 0, slot]
        lat = number // (2 * east) - az * north
        lon = number % (2 * east) - rg * east
        inside = (number >= 0) & (lat >= 0) & (lat < north)
        at_edge = (lon < 0) | (lon >= east)
        place = jnp.where(at_edge, north * east + lat, lat * east + lon)
        return extended[jnp.where(inside, place, north * east + north)]

    copies = []
    for d in range(1, count_az):
        for slot in range(slots):
            outgoing[d - 1, slot] = pick(d, slot)
        device = {"az": lax.rem(az + count_az - d, count_az), "rg": rg}
        copy = remote(
            outgoing.at[d - 1], incoming.at[d - 1], block_send.at[d - 1], block_recv.at[d - 1], device
        )
        copy.start()
        copies.append(copy)
    for slot in range(slots):
        table_ref[slot] = pick(0, slot)
    for d, copy in enumerate(copies):
        copy.wait()
        table_ref[...] += incoming[d]


def halo_kernel(count_az, rim, flat_ref, padded_ref, top, bottom, side, top_side, bottom_side, send, recv):
    az, rg = lax.axis_index("az"), lax.axis_index("rg")
    lines, samples = flat_ref.shape[1:]
    partner = {"az": az, "rg": 1 - rg}
    above, below = az - 1, az + 1
    barrier = pltpu.get_barrier_semaphore()

    def signal(device):
        pl.semaphore_signal(barrier, inc=1, device_id=device, device_id_type=MESH)

    edge = pl.ds(pl.multiple_of((1 - rg) * (samples - LANES), LANES), LANES)
    first, last = pl.ds(0, rim), pl.ds(lines - rim, rim)
    side_copy = remote(flat_ref.at[:, :, edge], side, send.at[0], recv.at[0], partner)
    up = [
        remote(flat_ref.at[:, first, :], bottom, send.at[1], recv.at[2], {"az": above, "rg": rg}),
        remote(
            flat_ref.at[:, first, edge], bottom_side, send.at[2], recv.at[4], {"az": above, "rg": 1 - rg}
        ),
    ]
    down = [
        remote(flat_ref.at[:, last, :], top, send.at[3], recv.at[1], {"az": below, "rg": rg}),
        remote(
            flat_ref.at[:, last, edge], top_side, send.at[4], recv.at[3], {"az": below, "rg": 1 - rg}
        ),
    ]
    signal(partner)

    @pl.when(az > 0)
    def _():
        signal({"az": above, "rg": rg})
        signal({"az": above, "rg": 1 - rg})

    @pl.when(az < count_az - 1)
    def _():
        signal({"az": below, "rg": rg})
        signal({"az": below, "rg": 1 - rg})

    has_above = (az > 0).astype(jnp.int32)
    has_below = (az < count_az - 1).astype(jnp.int32)
    pl.semaphore_wait(barrier, 1 + 2 * has_above + 2 * has_below)

    @pl.when(az > 0)
    def _():
        for copy in up:
            copy.start()

    @pl.when(az < count_az - 1)
    def _():
        for copy in down:
            copy.start()

    side_copy.start()

    def place(rows, centre, beside):
        left = jnp.where(rg == 1, beside, 0.0)
        right = jnp.where(rg == 0, beside, 0.0)
        for part in range(2):
            wide = jnp.concatenate([left[part], centre[part], right[part]], axis=1)
            padded_ref[part, rows, :] = wide[:, LANES - rim : 2 * LANES - rim + samples]

    side_copy.wait()
    place(slice(rim, rim + lines), flat_ref[...], side[...])

    @pl.when(az > 0)
    def _():
        for copy in up:
            copy.wait_send()

    @pl.when(az < count_az - 1)
    def _():
        for copy in down:
            copy.wait_send()

    @pl.when(az > 0)
    def _():
        for copy in down:
            copy.wait_recv()
        place(slice(0, rim), top[...], top_side[...])

    @pl.when(az == 0)
    def _():
        padded_ref[:, :rim, :] = jnp.zeros((2, rim, padded_ref.shape[2]), F32)

    @pl.when(az < count_az - 1)
    def _():
        for copy in up:
            copy.wait_recv()
        place(slice(rim + lines, 2 * rim + lines), bottom[...], bottom_side[...])

    @pl.when(az == count_az - 1)
    def _():
        padded_ref[:, rim + lines :, :] = jnp.zeros((2, rim, padded_ref.shape[2]), F32)


def reduce_kernel(count_az, sums_ref, out_ref, half, near, far, near_send, near_recv, far_send, far_recv):
    channels, rows, lanes = half.shape
    tile = rows // count_az
    az, rg, others, partner = peers(count_az)
    greet(others + [partner])
    mine = pl.ds(pl.multiple_of(rg * lanes, LANES), lanes)
    theirs = pl.ds(pl.multiple_of((1 - rg) * lanes, LANES), lanes)
    near_copies = [
        remote(sums_ref.at[c, :, theirs], near.at[c], near_send.at[c], near_recv.at[c], partner)
        for c in range(channels)
    ]
    for copy in near_copies:
        copy.start()
    for c, copy in enumerate(near_copies):
        copy.wait()
        half[c] = sums_ref[c, :, mine] + near[c]
    copies = []
    for d, device in enumerate(others):
        start = pl.multiple_of(device["az"] * tile, 8)
        copy = remote(
            half.at[:, pl.ds(start, tile), :], far.at[d], far_send.at[d], far_recv.at[d], device
        )
        copy.start()
        copies.append(copy)
    total = half[:, pl.ds(pl.multiple_of(az * tile, 8), tile), :]
    for d, copy in enumerate(copies):
        copy.wait()
        total = total + far[d]
    out_ref[...] = total[:2] / jnp.maximum(total[2:3], 1.0)


def body(
    complex_phase_image,
    phase_to_topography_factor,
    terrain_model_heights,
    radar_parcel_listing,
    pixel_terrain_position,
    multilook_receiving_patch,
    multilook_base_point,
    multilook_splat_shares,
):
    count_az = lax.axis_size("az")
    count_rg = lax.axis_size("rg")
    assert count_rg == 2
    north, east, points = terrain_model_heights.shape
    slots = radar_parcel_listing.shape[1]
    az_lines, rg_samples = phase_to_topography_factor.shape
    dma = pltpu.SemaphoreType.DMA
    block = (points // LANES, LANES)
    listing = jnp.broadcast_to(jnp.pad(radar_parcel_listing, ((0, 0), (0, LANES - slots))), (8, LANES))
    table = pl.pallas_call(
        functools.partial(terrain_kernel, count_az, (north, east)),
        out_shape=jax.ShapeDtypeStruct((slots,) + block, F32),
        scratch_shapes=[
            pltpu.VMEM((north * east + north + 1,) + block, F32),
            pltpu.VMEM((north,) + block, F32),
            pltpu.VMEM((count_az, 8, LANES), jnp.int32),
            pltpu.SMEM((count_az, 8, LANES), jnp.int32),
            pltpu.VMEM((count_az - 1, slots) + block, F32),
            pltpu.VMEM((count_az - 1, slots) + block, F32),
            dma((2,)),
            dma((count_az - 1,)),
            dma((count_az - 1,)),
            dma((count_az - 1,)),
            dma((count_az - 1,)),
            dma,
        ],
        compiler_params=pltpu.CompilerParams(collective_id=0, has_side_effects=True),
        name="terrain",
    )(listing, terrain_model_heights.reshape((north * east,) + block))
    flattened = pl.pallas_call(
        flatten_tile,
        out_shape=jax.ShapeDtypeStruct((2, az_lines, rg_samples), F32),
        name="flatten",
    )(
        complex_phase_image,
        phase_to_topography_factor,
        pixel_terrain_position,
        table.reshape(-1, LANES),
    )
    rim = PATCH // 4
    padded = pl.pallas_call(
        functools.partial(halo_kernel, count_az, rim),
        out_shape=jax.ShapeDtypeStruct((2, az_lines + 2 * rim, rg_samples + LANES), F32),
        in_specs=[pl.BlockSpec(memory_space=pltpu.VMEM)],
        scratch_shapes=[
            pltpu.VMEM((2, rim, rg_samples), F32),
            pltpu.VMEM((2, rim, rg_samples), F32),
            pltpu.VMEM((2, az_lines, LANES), F32),
            pltpu.VMEM((2, rim, LANES), F32),
            pltpu.VMEM((2, rim, LANES), F32),
            dma((5,)),
            dma((5,)),
        ],
        compiler_params=pltpu.CompilerParams(collective_id=1, has_side_effects=True),
        name="halo",
    )(flattened)
    map_lat = az_lines // LOOK
    map_lon = rg_samples // LOOK
    chunks = map_lat * map_lon // LANES
    tables = filter_tables()
    sums = pl.pallas_call(
        functools.partial(filter_kernel, (map_lat, map_lon)),
        out_shape=jax.ShapeDtypeStruct((3, map_lat * count_az, map_lon * count_rg), F32),
        scratch_shapes=[
            pltpu.VMEM((2, map_lat * count_az, chunks * LANES), F32),
            pltpu.VMEM((map_lon * count_rg, chunks * LANES), BF16),
        ],
        compiler_params=pltpu.CompilerParams(vmem_limit_bytes=48 * 1024 * 1024),
        name="filter_splat",
    )(
        padded,
        multilook_receiving_patch.reshape(chunks, LANES),
        multilook_base_point.reshape(chunks, LANES),
        multilook_splat_shares.reshape(4, chunks, LANES),
        *tables,
    )
    return pl.pallas_call(
        functools.partial(reduce_kernel, count_az),
        out_shape=jax.ShapeDtypeStruct((2, map_lat, map_lon), F32),
        in_specs=[pl.BlockSpec(memory_space=pltpu.VMEM)],
        scratch_shapes=[
            pltpu.VMEM((3, map_lat * count_az, map_lon), F32),
            pltpu.VMEM((3, map_lat * count_az, map_lon), F32),
            pltpu.VMEM((count_az - 1, 3, map_lat, map_lon), F32),
            dma((3,)),
            dma((3,)),
            dma((count_az - 1,)),
            dma((count_az - 1,)),
        ],
        compiler_params=pltpu.CompilerParams(
            collective_id=2, has_side_effects=True, vmem_limit_bytes=48 * 1024 * 1024
        ),
        name="reduce",
    )(sums)


def solution(mesh):
    return jax.shard_map(
        body,
        mesh=mesh,
        in_specs=(
            P(None, ("scene", "az"), "rg"),
            P(("scene", "az"), "rg"),
            P(("scene", "az"), "rg", None),
            P(("scene", "az", "rg"), None),
            P(("scene", "az"), "rg"),
            P(("scene", "az", "rg"), None),
            P(("scene", "az", "rg")),
            P(None, ("scene", "az", "rg")),
        ),
        out_specs=P(None, ("scene", "az"), "rg"),
        check_vma=False,
    )
```

```python
import functools
import math

import jax
import jax.numpy as jnp
import numpy as np
from jax import lax
from jax.experimental import pallas as pl
from jax.experimental.pallas import tpu as pltpu
from jax.sharding import PartitionSpec as P

PATCH = 64
LOOK = 4
LANES = 128
EPS = 1e-06
F32 = jnp.float32
BF16 = jnp.bfloat16


def halves(value):
    high = value.astype(BF16)
    return high, (value - high.astype(F32)).astype(BF16)


def dot3(left, right):
    left_high, left_low = left
    right_high, right_low = right
    out = jnp.dot(left_high, right_high, preferred_element_type=F32)
    out = out + jnp.dot(left_low, right_high, preferred_element_type=F32)
    return out + jnp.dot(left_high, right_low, preferred_element_type=F32)


def filter_tables():
    steps = np.arange(PATCH)
    angle = (steps[:, None] * steps[None, :] % PATCH) * (2.0 * math.pi / PATCH)
    cosine, sine = np.cos(angle), np.sin(angle)
    left = np.block([[cosine, sine], [-sine, cosine]])
    step, wide = PATCH // 2, 4 * PATCH
    right = np.zeros((2 * wide, 2 * wide))
    for p in range(4):
        rows, cols = slice(p * step, p * step + PATCH), slice(p * PATCH, (p + 1) * PATCH)
        rows_im = slice(wide + p * step, wide + p * step + PATCH)
        cols_im = slice(wide + p * PATCH, wide + (p + 1) * PATCH)
        right[rows, cols] = cosine
        right[rows, cols_im] = -sine
        right[rows_im, cols] = sine
        right[rows_im, cols_im] = cosine
    group = np.arange(wide) // PATCH
    same = group[:, None] == group[None, :]
    gap = (np.arange(wide)[:, None] - np.arange(wide)[None, :]) % PATCH
    band = same & ((gap <= 1) | (gap == PATCH - 1))
    cells = PATCH // 2 // LOOK
    places = PATCH // 4 + np.arange(cells * LOOK)
    turn = steps[:, None] * places[None, :] % PATCH * (2.0 * math.pi / PATCH)
    mean_re = np.cos(turn).reshape(PATCH, cells, LOOK).mean(axis=2) / PATCH
    mean_im = np.sin(turn).reshape(PATCH, cells, LOOK).mean(axis=2) / PATCH
    back_left = np.block([[mean_re.T, -mean_im.T], [mean_im.T, mean_re.T]])
    back_right = np.zeros((2 * wide, 8 * cells))
    for p in range(4):
        rows = slice(p * PATCH, (p + 1) * PATCH)
        rows_im = slice(wide + p * PATCH, wide + (p + 1) * PATCH)
        cols = slice(p * cells, (p + 1) * cells)
        cols_im = slice((4 + p) * cells, (5 + p) * cells)
        back_right[rows, cols] = mean_re
        back_right[rows, cols_im] = mean_im
        back_right[rows_im, cols] = -mean_im
        back_right[rows_im, cols_im] = mean_re
    tables = []
    for table in (left, right, back_left, back_right):
        high = table.astype(np.float32).astype(jnp.bfloat16)
        tables += [high, (table - high.astype(np.float64)).astype(jnp.bfloat16)]
    return tables + [band.astype(jnp.bfloat16), same.astype(jnp.bfloat16)]


def sine_cosine(angle):
    turns = jnp.floor(angle * (2.0 / math.pi) + 0.5)
    rest = angle - turns * 1.5703125
    rest = rest - turns * 4.837512969970703e-04
    rest = rest - turns * 7.549789948768648e-08
    square = rest * rest
    sine = ((-1.9515295891e-4 * square + 8.3321608736e-3) * square - 1.6666654611e-1) * square
    sine = sine * rest + rest
    cosine = ((2.443315711809948e-5 * square - 1.388731625493765e-3) * square + 4.166664568298827e-2)
    cosine = cosine * square * square - 0.5 * square + 1.0
    quarter = turns.astype(jnp.int32) & 3
    swap = (quarter & 1) == 1
    sine_out = jnp.where(swap, cosine, sine)
    cosine_out = jnp.where(swap, sine, cosine)
    sine_out = jnp.where(quarter >= 2, -sine_out, sine_out)
    cosine_out = jnp.where((quarter == 1) | (quarter == 2), -cosine_out, cosine_out)
    return sine_out, cosine_out


def goldstein_looks(padded, tables):
    left = (tables[0][...], tables[1][...])
    right = (tables[2], tables[3])
    back_left = (tables[4][...], tables[5][...])
    back_right = (tables[6], tables[7])
    band, same = tables[8][...], tables[9][...]
    step, wide = PATCH // 2, 4 * PATCH
    lines, samples = padded.shape[1:]
    block_rows = (lines - step) // step
    groups = (samples - LANES) // LANES
    columns = []
    for u in range(block_rows):
        strip = jnp.concatenate(
            [padded[0, u * step : u * step + PATCH], padded[1, u * step : u * step + PATCH]], axis=0
        )
        columns.append(dot3(left, halves(strip)))
    real = halves(jnp.concatenate([c[:PATCH] for c in columns], axis=0))
    imag = halves(jnp.concatenate([c[PATCH:] for c in columns], axis=0))
    rows_re, rows_im = [], []
    for q in range(groups):
        window = slice(q * LANES, q * LANES + wide)
        spectrum = dot3(
            (real[0][:, window], real[1][:, window]), (right[0][:wide], right[1][:wide])
        ) + dot3((imag[0][:, window], imag[1][:, window]), (right[0][wide:], right[1][wide:]))
        spec_re, spec_im = spectrum[:, :wide], spectrum[:, wide:]
        size = jnp.sqrt(spec_re * spec_re + spec_im * spec_im)
        size_high, size_low = halves(size)
        across = jnp.dot(size_high, band, preferred_element_type=F32) + jnp.dot(
            size_low, band, preferred_element_type=F32
        )
        gains = []
        for u in range(block_rows):
            part = across[u * PATCH : (u + 1) * PATCH]
            around = part + pltpu.roll(part, 1, 0) + pltpu.roll(part, PATCH - 1, 0)
            column = jnp.sum(size[u * PATCH : (u + 1) * PATCH], axis=0, keepdims=True)
            column_high, column_low = halves(jnp.broadcast_to(column, (16, wide)))
            total = jnp.dot(column_high, same, preferred_element_type=F32) + jnp.dot(
                column_low, same, preferred_element_type=F32
            )
            scale = (1.0 / 9.0) / (total[:1] * (1.0 / PATCH**2) + EPS)
            gains.append(jnp.sqrt(around * scale))
        gain = jnp.concatenate(gains, axis=0)
        rows = dot3(halves(spec_re * gain), (back_right[0][:wide], back_right[1][:wide])) + dot3(
            halves(spec_im * gain), (back_right[0][wide:], back_right[1][wide:])
        )
        half = rows.shape[1] // 2
        rows_re.append(rows[:, :half])
        rows_im.append(rows[:, half:])
    rows_re = jnp.concatenate(rows_re, axis=1)
    rows_im = jnp.concatenate(rows_im, axis=1)
    looks = []
    for u in range(block_rows):
        rows = slice(u * PATCH, (u + 1) * PATCH)
        looks.append(dot3(back_left, halves(jnp.concatenate([rows_re[rows], rows_im[rows]], axis=0))))
    half = looks[0].shape[0] // 2
    return [jnp.concatenate([x[:half] for x in looks], axis=0), jnp.concatenate([x[half:] for x in looks], axis=0)]


def place_looks(owner_ref, base_ref, share_ref, row_ref, hit_ref, map_lat, map_lon, tile_lat, tile_lon):
    chunks = owner_ref.shape[0]
    count_rg = map_lon // tile_lon
    owner, base = owner_ref[...], base_ref[...]
    anchor_row = owner // count_rg * tile_lat + base // tile_lon
    anchor_col = owner % count_rg * tile_lon + base % tile_lon
    row_ids = lax.broadcasted_iota(jnp.int32, (map_lat, LANES), 0)
    col_ids = lax.broadcasted_iota(jnp.int32, (map_lon, LANES), 0)
    for i in range(chunks):
        span = slice(i * LANES, (i + 1) * LANES)
        hit_ref[:, span] = (col_ids == anchor_col[i : i + 1]).astype(F32).astype(BF16)
        gap = row_ids - anchor_row[i : i + 1]
        for c in range(2):
            upper, lower = share_ref[c, i : i + 1, :], share_ref[2 + c, i : i + 1, :]
            row_ref[c, :, span] = jnp.where(gap == 0, upper, jnp.where(gap == 1, lower, 0.0))


def splat(row_ref, hit_ref, look):
    dims = (((1,), (1,)), ((), ()))
    chunks = hit_ref.shape[1] // LANES
    sums = []
    for c in range(2):
        if look is None:
            value = row_ref[c]
        else:
            value = jnp.concatenate(
                [row_ref[c, :, i * LANES : (i + 1) * LANES] * look[i : i + 1] for i in range(chunks)],
                axis=1,
            )
        high, low = halves(value)
        sums.append(
            lax.dot_general(high, hit_ref[...], dims, preferred_element_type=F32)
            + lax.dot_general(low, hit_ref[...], dims, preferred_element_type=F32)
        )
    moved = pltpu.roll(sums[1], 1, 1)
    first = lax.broadcasted_iota(jnp.int32, moved.shape, 1) == 0
    return sums[0] + jnp.where(first, 0.0, moved)


MESH = pl.DeviceIdType.MESH


def peers(count_az):
    az, rg = lax.axis_index("az"), lax.axis_index("rg")
    others = [{"az": lax.rem(az + d, count_az), "rg": rg} for d in range(1, count_az)]
    return az, rg, others, {"az": az, "rg": 1 - rg}


def greet(devices):
    barrier = pltpu.get_barrier_semaphore()
    for device in devices:
        pl.semaphore_signal(barrier, inc=1, device_id=device, device_id_type=MESH)
    pl.semaphore_wait(barrier, len(devices))


def remote(source, target, send_sem, recv_sem, device):
    return pltpu.make_async_remote_copy(
        src_ref=source,
        dst_ref=target,
        send_sem=send_sem,
        recv_sem=recv_sem,
        device_id=device,
        device_id_type=MESH,
    )


def look_up(table_ref, heights_ref, lane_ref, row_ref, lines, rows, fresh):
    count = lines.stop - lines.start

    def one_column(column, carry):
        span = pl.ds(pl.multiple_of(column * LANES, LANES), LANES)
        lane, row = lane_ref[lines, span], row_ref[lines, span]
        heights = jnp.zeros((count, LANES), F32) if fresh else heights_ref[lines, span]
        for r in rows:
            source = jnp.broadcast_to(table_ref[r // 8, r % 8 : r % 8 + 1, :], (count, LANES))
            picked = jnp.take_along_axis(source, lane, axis=1, mode="promise_in_bounds")
            heights = jnp.where(row == r, picked, heights)
        heights_ref[lines, span] = heights
        return carry

    lax.fori_loop(0, heights_ref.shape[1] // LANES, one_column, 0)


def flatten_lines(image_ref, factor_ref, heights_ref, flat_ref, lines):
    sine, cosine = sine_cosine(factor_ref[lines, :] * heights_ref[lines, :])
    real, imag = image_ref[0, lines, :], image_ref[1, lines, :]
    flat_ref[0, lines, :] = real * cosine + imag * sine
    flat_ref[1, lines, :] = imag * cosine - real * sine


def flat_kernel(
    count_az,
    rim,
    slot_groups,
    list_ref,
    terrain_ref,
    position_ref,
    factor_ref,
    image_ref,
    padded_ref,
    extended,
    edge,
    own_list,
    lists,
    lists_smem,
    outgoing,
    incoming,
    table_ref,
    heights_ref,
    lane_ref,
    row_ref,
    flat_ref,
    top,
    bottom,
    side,
    top_side,
    bottom_side,
    edge_sems,
    list_send,
    list_recv,
    block_send,
    block_recv,
    local_sem,
    send,
    recv,
):
    north, east = terrain_ref.shape[:2]
    slots = list_ref.shape[1]
    block = extended.shape[1:]
    lines, samples = factor_ref.shape
    az, rg, others, partner = peers(count_az)
    barrier = pltpu.get_barrier_semaphore()
    crossed = [
        {"az": lax.rem(az + d, count_az), "rg": 1 - rg} for d in (1, count_az - 1)
    ]
    greeted = others + [partner] + crossed
    for device in greeted:
        pl.semaphore_signal(barrier, inc=1, device_id=device, device_id_type=MESH)
    own_list[...] = jnp.full(own_list.shape, -1, jnp.int32)
    own_list[0:1, 0:slots] = list_ref[...]
    lists[0] = own_list[...]
    for lat in range(north):
        extended[lat * east : (lat + 1) * east] = terrain_ref[lat].reshape((east,) + block)
    extended[north * east + north] = jnp.zeros(block, F32)
    for lat in range(north):
        edge[lat] = jnp.where(rg == 0, extended[lat * east + east - 1], extended[lat * east])
    pl.semaphore_wait(barrier, len(greeted))
    list_copies = [
        remote(own_list, lists.at[d + 1], list_send.at[d], list_recv.at[d], device)
        for d, device in enumerate(others)
    ]
    for copy in list_copies:
        copy.start()
    edge_copy = remote(
        edge, extended.at[pl.ds(north * east, north)], edge_sems.at[0], edge_sems.at[1], partner
    )
    edge_copy.start()
    position = position_ref[...]
    lane_ref[...] = position & (LANES - 1)
    row_ref[...] = lax.shift_right_logical(position, LANES.bit_length() - 1)
    for copy in list_copies:
        copy.wait()
    to_smem = pltpu.make_async_copy(lists, lists_smem, local_sem)
    to_smem.start()
    edge_copy.wait()
    to_smem.wait()

    def pick(d, slot):
        number = lists_smem[d, 0, slot]
        lat = number // (2 * east) - az * north
        lon = number % (2 * east) - rg * east
        inside = (number >= 0) & (lat >= 0) & (lat < north)
        at_edge = (lon < 0) | (lon >= east)
        place = jnp.where(at_edge, north * east + lat, lat * east + lon)
        return extended[jnp.where(inside, place, north * east + north)]

    copies = []
    for g, group in enumerate(slot_groups):
        span = pl.ds(group.start, len(group))
        for d in range(1, count_az):
            for slot in group:
                outgoing[d - 1, slot] = pick(d, slot)
            device = {"az": lax.rem(az + count_az - d, count_az), "rg": rg}
            copy = remote(
                outgoing.at[d - 1, span],
                incoming.at[d - 1, span],
                block_send.at[g, d - 1],
                block_recv.at[g, d - 1],
                device,
            )
            copy.start()
            copies.append(copy)
    for slot in range(slots):
        table_ref[slot] = pick(0, slot)
    first, middle, last = slice(0, rim), slice(rim, lines - rim), slice(lines - rim, lines)
    for g, group in enumerate(slot_groups):
        span = slice(group.start, group.stop)
        total = table_ref[span]
        for d in range(count_az - 1):
            copies[g * (count_az - 1) + d].wait()
            total = total + incoming[d, span]
        table_ref[span] = total
        rows = range(group.start * block[0], group.stop * block[0])
        if g < len(slot_groups) - 1:
            look_up(table_ref, heights_ref, lane_ref, row_ref, slice(0, lines), rows, g == 0)
        else:
            look_up(table_ref, heights_ref, lane_ref, row_ref, first, rows, g == 0)
            look_up(table_ref, heights_ref, lane_ref, row_ref, last, rows, g == 0)
    for part in (first, last):
        flatten_lines(image_ref, factor_ref, heights_ref, flat_ref, part)
    beside = pl.ds(pl.multiple_of((1 - rg) * (samples - LANES), LANES), LANES)
    first_ds, last_ds = pl.ds(0, rim), pl.ds(lines - rim, rim)
    above, below = az - 1, az + 1
    up = [
        remote(flat_ref.at[:, first_ds, :], bottom, send.at[1], recv.at[2], {"az": above, "rg": rg}),
        remote(
            flat_ref.at[:, first_ds, beside], bottom_side, send.at[2], recv.at[4], {"az": above, "rg": 1 - rg}
        ),
    ]
    down = [
        remote(flat_ref.at[:, last_ds, :], top, send.at[3], recv.at[1], {"az": below, "rg": rg}),
        remote(
            flat_ref.at[:, last_ds, beside], top_side, send.at[4], recv.at[3], {"az": below, "rg": 1 - rg}
        ),
    ]

    @pl.when(az > 0)
    def _():
        for copy in up:
            copy.start()

    @pl.when(az < count_az - 1)
    def _():
        for copy in down:
            copy.start()

    look_up(table_ref, heights_ref, lane_ref, row_ref, middle, rows, len(slot_groups) == 1)
    flatten_lines(image_ref, factor_ref, heights_ref, flat_ref, middle)
    side_copy = remote(flat_ref.at[:, :, beside], side, send.at[0], recv.at[0], partner)
    side_copy.start()

    def place(target, centre, nearby):
        left = jnp.where(rg == 1, nearby, 0.0)
        right = jnp.where(rg == 0, nearby, 0.0)
        for part in range(2):
            wide = jnp.concatenate([left[part], centre[part], right[part]], axis=1)
            padded_ref[part, target, :] = wide[:, LANES - rim : 2 * LANES - rim + samples]

    side_copy.wait()
    place(slice(rim, rim + lines), flat_ref[...], side[...])

    @pl.when(az > 0)
    def _():
        for copy in up:
            copy.wait_send()

    @pl.when(az < count_az - 1)
    def _():
        for copy in down:
            copy.wait_send()

    @pl.when(az > 0)
    def _():
        for copy in down:
            copy.wait_recv()
        place(slice(0, rim), top[...], top_side[...])

    @pl.when(az == 0)
    def _():
        padded_ref[:, :rim, :] = jnp.zeros((2, rim, padded_ref.shape[2]), F32)

    @pl.when(az < count_az - 1)
    def _():
        for copy in up:
            copy.wait_recv()
        place(slice(rim + lines, 2 * rim + lines), bottom[...], bottom_side[...])

    @pl.when(az == count_az - 1)
    def _():
        padded_ref[:, rim + lines :, :] = jnp.zeros((2, rim, padded_ref.shape[2]), F32)


def map_kernel(count_az, padded_ref, owner_ref, base_ref, share_ref, *refs):
    tables, refs = refs[:10], refs[10:]
    out_ref, row_ref, hit_ref, sums_ref, half, near, far, near_send, near_recv, far_send, far_recv = refs
    channels, map_lat, map_lon = sums_ref.shape
    tile, lanes = out_ref.shape[1:]
    az, rg, others, partner = peers(count_az)
    barrier = pltpu.get_barrier_semaphore()
    for device in others + [partner]:
        pl.semaphore_signal(barrier, inc=1, device_id=device, device_id_type=MESH)
    mine = pl.ds(pl.multiple_of(rg * lanes, LANES), lanes)
    theirs = pl.ds(pl.multiple_of((1 - rg) * lanes, LANES), lanes)
    near_copies = [
        remote(sums_ref.at[c, :, theirs], near.at[c], near_send.at[c], near_recv.at[c], partner)
        for c in range(channels)
    ]
    far_copies = [
        [
            remote(
                half.at[c, pl.ds(pl.multiple_of(device["az"] * tile, 8), tile), :],
                far.at[c, d],
                far_send.at[c, d],
                far_recv.at[c, d],
                device,
            )
            for d, device in enumerate(others)
        ]
        for c in range(channels)
    ]

    def spread(c):
        near_copies[c].wait()
        half[c] = sums_ref[c, :, mine] + near[c]
        for copy in far_copies[c]:
            copy.start()

    def gathered(c):
        total = half[c, pl.ds(pl.multiple_of(az * tile, 8), tile), :]
        for d, copy in enumerate(far_copies[c]):
            copy.wait()
            total = total + far[c, d]
        return total

    place_looks(owner_ref, base_ref, share_ref, row_ref, hit_ref, map_lat, map_lon, tile, lanes)
    sums_ref[2] = splat(row_ref, hit_ref, None)
    pl.semaphore_wait(barrier, len(others) + 1)
    near_copies[2].start()
    looks = goldstein_looks(padded_ref, tables)
    spread(2)
    sums_ref[0] = splat(row_ref, hit_ref, looks[0])
    near_copies[0].start()
    sums_ref[1] = splat(row_ref, hit_ref, looks[1])
    near_copies[1].start()
    spread(0)
    spread(1)
    weight = jnp.maximum(gathered(2), 1.0)
    out_ref[0] = gathered(0) / weight
    out_ref[1] = gathered(1) / weight


def body(
    complex_phase_image,
    phase_to_topography_factor,
    terrain_model_heights,
    radar_parcel_listing,
    pixel_terrain_position,
    multilook_receiving_patch,
    multilook_base_point,
    multilook_splat_shares,
):
    count_az = lax.axis_size("az")
    count_rg = lax.axis_size("rg")
    assert count_rg == 2
    north, east, points = terrain_model_heights.shape
    slots = radar_parcel_listing.shape[1]
    az_lines, rg_samples = phase_to_topography_factor.shape
    dma = pltpu.SemaphoreType.DMA
    block = (points // LANES, LANES)
    rim = PATCH // 4
    groups = [range(start, min(start + 3, slots)) for start in range(0, slots, 3)]
    tile = (az_lines, rg_samples)
    padded = pl.pallas_call(
        functools.partial(flat_kernel, count_az, rim, groups),
        out_shape=jax.ShapeDtypeStruct((2, az_lines + 2 * rim, rg_samples + LANES), F32),
        in_specs=[pl.BlockSpec(memory_space=pltpu.VMEM)] * 5,
        scratch_shapes=[
            pltpu.VMEM((north * east + north + 1,) + block, F32),
            pltpu.VMEM((north,) + block, F32),
            pltpu.VMEM((8, LANES), jnp.int32),
            pltpu.VMEM((count_az, 8, LANES), jnp.int32),
            pltpu.SMEM((count_az, 8, LANES), jnp.int32),
            pltpu.VMEM((count_az - 1, slots) + block, F32),
            pltpu.VMEM((count_az - 1, slots) + block, F32),
            pltpu.VMEM((slots,) + block, F32),
            pltpu.VMEM(tile, F32),
            pltpu.VMEM(tile, jnp.int32),
            pltpu.VMEM(tile, jnp.int32),
            pltpu.VMEM((2,) + tile, F32),
            pltpu.VMEM((2, rim, rg_samples), F32),
            pltpu.VMEM((2, rim, rg_samples), F32),
            pltpu.VMEM((2, az_lines, LANES), F32),
            pltpu.VMEM((2, rim, LANES), F32),
            pltpu.VMEM((2, rim, LANES), F32),
            dma((2,)),
            dma((count_az - 1,)),
            dma((count_az - 1,)),
            dma((len(groups), count_az - 1)),
            dma((len(groups), count_az - 1)),
            dma,
            dma((5,)),
            dma((5,)),
        ],
        compiler_params=pltpu.CompilerParams(
            collective_id=0, has_side_effects=True, vmem_limit_bytes=32 * 1024 * 1024
        ),
        name="flat",
    )(
        radar_parcel_listing,
        terrain_model_heights,
        pixel_terrain_position,
        phase_to_topography_factor,
        complex_phase_image,
    )
    map_lat = az_lines // LOOK
    map_lon = rg_samples // LOOK
    chunks = map_lat * map_lon // LANES
    whole_lat, whole_lon = map_lat * count_az, map_lon * count_rg
    tables = filter_tables()
    return pl.pallas_call(
        functools.partial(map_kernel, count_az),
        out_shape=jax.ShapeDtypeStruct((2, map_lat, map_lon), F32),
        in_specs=[pl.BlockSpec(memory_space=pltpu.VMEM)] * 14,
        scratch_shapes=[
            pltpu.VMEM((2, whole_lat, chunks * LANES), F32),
            pltpu.VMEM((whole_lon, chunks * LANES), BF16),
            pltpu.VMEM((3, whole_lat, whole_lon), F32),
            pltpu.VMEM((3, whole_lat, map_lon), F32),
            pltpu.VMEM((3, whole_lat, map_lon), F32),
            pltpu.VMEM((3, count_az - 1, map_lat, map_lon), F32),
            dma((3,)),
            dma((3,)),
            dma((3, count_az - 1)),
            dma((3, count_az - 1)),
        ],
        compiler_params=pltpu.CompilerParams(
            collective_id=1, has_side_effects=True, vmem_limit_bytes=48 * 1024 * 1024
        ),
        name="filter_map",
    )(
        padded,
        multilook_receiving_patch.reshape(chunks, LANES),
        multilook_base_point.reshape(chunks, LANES),
        multilook_splat_shares.reshape(4, chunks, LANES),
        *tables,
    )


def solution(mesh):
    return jax.shard_map(
        body,
        mesh=mesh,
        in_specs=(
            P(None, ("scene", "az"), "rg"),
            P(("scene", "az"), "rg"),
            P(("scene", "az"), "rg", None),
            P(("scene", "az", "rg"), None),
            P(("scene", "az"), "rg"),
            P(("scene", "az", "rg"), None),
            P(("scene", "az", "rg")),
            P(None, ("scene", "az", "rg")),
        ),
        out_specs=P(None, ("scene", "az"), "rg"),
        check_vma=False,
    )
```

```python
import functools
import math

import jax
import jax.numpy as jnp
import numpy as np
from jax import lax
from jax.experimental import pallas as pl
from jax.experimental.pallas import tpu as pltpu
from jax.sharding import PartitionSpec as P

PATCH = 64
LOOK = 4
LANES = 128
EPS = 1e-06
F32 = jnp.float32
BF16 = jnp.bfloat16


def halves(value):
    high = value.astype(BF16)
    return high, (value - high.astype(F32)).astype(BF16)


def filter_tables():
    steps = np.arange(PATCH)
    angle = (steps[:, None] * steps[None, :] % PATCH) * (2.0 * math.pi / PATCH)
    cosine, sine = np.cos(angle), np.sin(angle)
    left = np.block([[cosine, sine], [-sine, cosine]])
    step, wide = PATCH // 2, 4 * PATCH
    right = np.zeros((2 * wide, 2 * wide))
    for p in range(4):
        rows, cols = slice(p * step, p * step + PATCH), slice(p * PATCH, (p + 1) * PATCH)
        rows_im = slice(wide + p * step, wide + p * step + PATCH)
        cols_im = slice(wide + p * PATCH, wide + (p + 1) * PATCH)
        right[rows, cols] = cosine
        right[rows, cols_im] = -sine
        right[rows_im, cols] = sine
        right[rows_im, cols_im] = cosine
    group = np.arange(wide) // PATCH
    same = group[:, None] == group[None, :]
    gap = (np.arange(wide)[:, None] - np.arange(wide)[None, :]) % PATCH
    band = same & ((gap <= 1) | (gap == PATCH - 1))
    cells = PATCH // 2 // LOOK
    places = PATCH // 4 + np.arange(cells * LOOK)
    turn = steps[:, None] * places[None, :] % PATCH * (2.0 * math.pi / PATCH)
    mean_re = np.cos(turn).reshape(PATCH, cells, LOOK).mean(axis=2) / PATCH
    mean_im = np.sin(turn).reshape(PATCH, cells, LOOK).mean(axis=2) / PATCH
    back_left = np.block([[mean_re.T, -mean_im.T], [mean_im.T, mean_re.T]])
    back_right = np.zeros((2 * wide, 8 * cells))
    for p in range(4):
        rows = slice(p * PATCH, (p + 1) * PATCH)
        rows_im = slice(wide + p * PATCH, wide + (p + 1) * PATCH)
        cols = slice(p * cells, (p + 1) * cells)
        cols_im = slice((4 + p) * cells, (5 + p) * cells)
        back_right[rows, cols] = mean_re
        back_right[rows, cols_im] = mean_im
        back_right[rows_im, cols] = -mean_im
        back_right[rows_im, cols_im] = mean_re
    tables = []
    for table in (left, right, back_left, back_right):
        high = table.astype(np.float32).astype(jnp.bfloat16)
        tables += [high, (table - high.astype(np.float64)).astype(jnp.bfloat16)]
    return tables + [band.astype(jnp.bfloat16), same.astype(jnp.bfloat16)]


def sine_cosine(angle):
    turns = jnp.floor(angle * (2.0 / math.pi) + 0.5)
    rest = angle - turns * 1.5703125
    rest = rest - turns * 4.837512969970703e-04
    rest = rest - turns * 7.549789948768648e-08
    square = rest * rest
    sine = ((-1.9515295891e-4 * square + 8.3321608736e-3) * square - 1.6666654611e-1) * square
    sine = sine * rest + rest
    cosine = ((2.443315711809948e-5 * square - 1.388731625493765e-3) * square + 4.166664568298827e-2)
    cosine = cosine * square * square - 0.5 * square + 1.0
    quarter = turns.astype(jnp.int32) & 3
    swap = (quarter & 1) == 1
    sine_out = jnp.where(swap, cosine, sine)
    cosine_out = jnp.where(swap, sine, cosine)
    sine_out = jnp.where(quarter >= 2, -sine_out, sine_out)
    cosine_out = jnp.where((quarter == 1) | (quarter == 2), -cosine_out, cosine_out)
    return sine_out, cosine_out


def stacked(left, right):
    rows = left.shape[0]
    high, low = halves(left)
    both = jnp.dot(jnp.concatenate([high, low], axis=0), right[0], preferred_element_type=F32)
    out = both[:rows] + both[rows:]
    if right[1] is None:
        return out
    return out + jnp.dot(high, right[1], preferred_element_type=F32)


def goldstein_looks(padded, tables):
    left_both = jnp.concatenate([tables[0][...], tables[1][...]], axis=0)
    back_both = jnp.concatenate([tables[4][...], tables[5][...]], axis=0)
    right = (tables[2], tables[3])
    back_right = (tables[6], tables[7])
    band, same = tables[8][...], tables[9][...]
    step, wide = PATCH // 2, 4 * PATCH
    lines, samples = padded.shape[1:]
    block_rows = (lines - step) // step
    groups = (samples - LANES) // LANES

    def table_first(both, value):
        rows = both.shape[0] // 2
        high, low = halves(value)
        first = jnp.dot(both, high, preferred_element_type=F32)
        return first[:rows] + first[rows:] + jnp.dot(both[:rows], low, preferred_element_type=F32)

    columns = []
    for u in range(block_rows):
        strip = jnp.concatenate(
            [padded[0, u * step : u * step + PATCH], padded[1, u * step : u * step + PATCH]], axis=0
        )
        columns.append(table_first(left_both, strip))
    windows = [slice(q * LANES, q * LANES + wide) for q in range(groups)]
    real = jnp.concatenate([c[:PATCH, w] for w in windows for c in columns], axis=0)
    imag = jnp.concatenate([c[PATCH:, w] for w in windows for c in columns], axis=0)
    spectrum = stacked(real, (right[0][:wide], right[1][:wide])) + stacked(
        imag, (right[0][wide:], right[1][wide:])
    )
    spec_re, spec_im = spectrum[:, :wide], spectrum[:, wide:]
    size = jnp.sqrt(spec_re * spec_re + spec_im * spec_im)
    across = stacked(size, (band, None))
    patches = groups * block_rows
    pieces = [slice(p * PATCH, (p + 1) * PATCH) for p in range(patches)]
    column_sums = jnp.concatenate(
        [jnp.sum(size[p], axis=0, keepdims=True) for p in pieces], axis=0
    )
    if patches % 16:
        column_sums = jnp.concatenate(
            [column_sums, jnp.zeros((16 - patches % 16, wide), F32)], axis=0
        )
    total = stacked(column_sums, (same, None))
    scale = (1.0 / 9.0) / (total * (1.0 / PATCH**2) + EPS)
    gains = []
    for p, piece in enumerate(pieces):
        part = across[piece]
        around = part + pltpu.roll(part, 1, 0) + pltpu.roll(part, PATCH - 1, 0)
        gains.append(jnp.sqrt(around * scale[p : p + 1]))
    gain = jnp.concatenate(gains, axis=0)
    rows = stacked(spec_re * gain, (back_right[0][:wide], back_right[1][:wide])) + stacked(
        spec_im * gain, (back_right[0][wide:], back_right[1][wide:])
    )
    half = rows.shape[1] // 2
    looks = []
    for u in range(block_rows):
        parts = [rows[pieces[q * block_rows + u]] for q in range(groups)]
        value = jnp.concatenate(
            [
                jnp.concatenate([x[:, :half] for x in parts], axis=1),
                jnp.concatenate([x[:, half:] for x in parts], axis=1),
            ],
            axis=0,
        )
        looks.append(table_first(back_both, value))
    half = looks[0].shape[0] // 2
    return [jnp.concatenate([x[:half] for x in looks], axis=0), jnp.concatenate([x[half:] for x in looks], axis=0)]


def anchors(owner, base, tile_lat, tile_lon, count_rg):
    row = owner // count_rg * tile_lat + base // tile_lon
    return row, owner % count_rg * tile_lon + base % tile_lon


def place_rows(anchor_row, share_ref, row_ref):
    row_ids = lax.broadcasted_iota(jnp.int32, (row_ref.shape[1], LANES), 0)
    for i in range(anchor_row.shape[0]):
        span = slice(i * LANES, (i + 1) * LANES)
        gap = row_ids - anchor_row[i : i + 1]
        for c in range(2):
            upper, lower = share_ref[c : c + 1, span], share_ref[2 + c : 3 + c, span]
            row_ref[c, :, span] = jnp.where(gap == 0, upper, jnp.where(gap == 1, lower, 0.0))


def place_columns(anchor_col, hit_ref):
    col_ids = lax.broadcasted_iota(jnp.int32, (LANES, hit_ref.shape[1]), 1).astype(F32)
    for i in range(anchor_col.shape[0]):
        column = jnp.broadcast_to(anchor_col[i : i + 1].astype(F32), (LANES, LANES)).T
        column = jnp.concatenate([column] * (hit_ref.shape[1] // LANES), axis=1)
        hit_ref[i * LANES : (i + 1) * LANES, :] = jnp.where(column == col_ids, 1.0, 0.0).astype(BF16)


def splat(row_ref, hit_ref, look):
    chunks = hit_ref.shape[0] // LANES
    rows = row_ref.shape[1]
    values = []
    for c in range(2):
        if look is None:
            value = row_ref[c]
        else:
            value = jnp.concatenate(
                [row_ref[c, :, i * LANES : (i + 1) * LANES] * look[i : i + 1] for i in range(chunks)],
                axis=1,
            )
        values += halves(value)
    sums = jnp.dot(jnp.concatenate(values, axis=0), hit_ref[...], preferred_element_type=F32)
    moved = pltpu.roll(sums[2 * rows : 3 * rows] + sums[3 * rows :], 1, 1)
    first = lax.broadcasted_iota(jnp.int32, moved.shape, 1) == 0
    return sums[:rows] + sums[rows : 2 * rows] + jnp.where(first, 0.0, moved)


MESH = pl.DeviceIdType.MESH


def peers(count_az):
    az, rg = lax.axis_index("az"), lax.axis_index("rg")
    others = [{"az": lax.rem(az + d, count_az), "rg": rg} for d in range(1, count_az)]
    return az, rg, others, {"az": az, "rg": 1 - rg}


def greet(devices):
    barrier = pltpu.get_barrier_semaphore()
    for device in devices:
        pl.semaphore_signal(barrier, inc=1, device_id=device, device_id_type=MESH)
    pl.semaphore_wait(barrier, len(devices))


def remote(source, target, send_sem, recv_sem, device):
    return pltpu.make_async_remote_copy(
        src_ref=source,
        dst_ref=target,
        send_sem=send_sem,
        recv_sem=recv_sem,
        device_id=device,
        device_id_type=MESH,
    )


def look_up(table_ref, heights_ref, lane_ref, row_ref, lines, rows, fresh):
    count = lines.stop - lines.start

    def one_column(column, carry):
        span = pl.ds(pl.multiple_of(column * LANES, LANES), LANES)
        lane, row = lane_ref[lines, span], row_ref[lines, span]
        heights = jnp.zeros((count, LANES), F32) if fresh else heights_ref[lines, span]
        for r in rows:
            source = jnp.broadcast_to(table_ref[r // 8, r % 8 : r % 8 + 1, :], (count, LANES))
            picked = jnp.take_along_axis(source, lane, axis=1, mode="promise_in_bounds")
            heights = jnp.where(row == r, picked, heights)
        heights_ref[lines, span] = heights
        return carry

    lax.fori_loop(0, heights_ref.shape[1] // LANES, one_column, 0)


def flatten_lines(image_ref, factor_ref, heights_ref, flat_ref, lines):
    sine, cosine = sine_cosine(factor_ref[lines, :] * heights_ref[lines, :])
    real, imag = image_ref[0, lines, :], image_ref[1, lines, :]
    flat_ref[0, lines, :] = real * cosine + imag * sine
    flat_ref[1, lines, :] = imag * cosine - real * sine


def whole_kernel(
    count_az,
    rim,
    slot_groups,
    *refs,
):
    sources, refs = refs[:18], refs[18:]
    out_ref, refs = refs[0], refs[1:]
    held, refs = refs[:18], refs[18:]
    list_ref, terrain_ref, position_ref, owner_ref, base_ref, share_ref, factor_ref, image_ref = held[:8]
    tables = held[8:]
    (
        load_sems,
        extended,
        edge,
        own_list,
        lists,
        lists_smem,
        outgoing,
        incoming,
        table_ref,
        heights_ref,
        lane_ref,
        row_ref,
        flat_ref,
        top,
        bottom,
        side,
        top_side,
        bottom_side,
        edge_sems,
        list_send,
        list_recv,
        block_send,
        block_recv,
        local_sem,
        send,
        recv,
        padded_ref,
        weight_ref,
        hit_ref,
        sums_ref,
        half,
        near,
        far,
        near_send,
        near_recv,
        far_send,
        far_recv,
    ) = refs
    north, east = terrain_ref.shape[:2]
    slots = list_ref.shape[1]
    block = extended.shape[1:]
    lines, samples = factor_ref.shape
    az, rg, others, partner = peers(count_az)
    barrier = pltpu.get_barrier_semaphore()
    crossed = [
        {"az": lax.rem(az + d, count_az), "rg": 1 - rg} for d in (1, count_az - 1)
    ]
    greeted = others + [partner] + crossed
    for device in greeted:
        pl.semaphore_signal(barrier, inc=1, device_id=device, device_id_type=MESH)
    loads = [
        pltpu.make_async_copy(source, target, load_sems.at[n])
        for n, (source, target) in enumerate(zip(sources, held))
    ]
    for load in loads:
        load.start()
    loads[0].wait()
    own_list[...] = jnp.full(own_list.shape, -1, jnp.int32)
    own_list[0:1, 0:slots] = list_ref[...]
    lists[0] = own_list[...]
    loads[1].wait()
    for lat in range(north):
        extended[lat * east : (lat + 1) * east] = terrain_ref[lat].reshape((east,) + block)
    extended[north * east + north] = jnp.zeros(block, F32)
    for lat in range(north):
        edge[lat] = jnp.where(rg == 0, extended[lat * east + east - 1], extended[lat * east])
    pl.semaphore_wait(barrier, len(greeted))
    list_copies = [
        remote(own_list, lists.at[d + 1], list_send.at[d], list_recv.at[d], device)
        for d, device in enumerate(others)
    ]
    for copy in list_copies:
        copy.start()
    edge_copy = remote(
        edge, extended.at[pl.ds(north * east, north)], edge_sems.at[0], edge_sems.at[1], partner
    )
    edge_copy.start()
    channels, map_lat, map_lon = sums_ref.shape
    tile, lanes = out_ref.shape[1:]
    mine = pl.ds(pl.multiple_of(rg * lanes, LANES), lanes)
    theirs = pl.ds(pl.multiple_of((1 - rg) * lanes, LANES), lanes)
    near_copies = [
        remote(sums_ref.at[c, :, theirs], near.at[c], near_send.at[c], near_recv.at[c], partner)
        for c in range(channels)
    ]
    far_copies = [
        [
            remote(
                half.at[c, pl.ds(pl.multiple_of(device["az"] * tile, 8), tile), :],
                far.at[c, d],
                far_send.at[c, d],
                far_recv.at[c, d],
                device,
            )
            for d, device in enumerate(others)
        ]
        for c in range(channels)
    ]

    def spread(c):
        near_copies[c].wait()
        half[c] = sums_ref[c, :, mine] + near[c]
        for copy in far_copies[c]:
            copy.start()

    def gathered(c):
        total = half[c, pl.ds(pl.multiple_of(az * tile, 8), tile), :]
        for d, copy in enumerate(far_copies[c]):
            copy.wait()
            total = total + far[c, d]
        return total

    loads[2].wait()
    position = position_ref[...]
    lane_ref[...] = position & (LANES - 1)
    row_ref[...] = lax.shift_right_logical(position, LANES.bit_length() - 1)
    for n in range(3, 6):
        loads[n].wait()
    anchor_row, anchor_col = anchors(owner_ref[...], base_ref[...], tile, lanes, map_lon // lanes)
    place_rows(anchor_row, share_ref, weight_ref)
    for copy in list_copies:
        copy.wait()
    to_smem = pltpu.make_async_copy(lists, lists_smem, local_sem)
    to_smem.start()
    edge_copy.wait()
    to_smem.wait()

    def pick(d, slot):
        number = lists_smem[d, 0, slot]
        lat = number // (2 * east) - az * north
        lon = number % (2 * east) - rg * east
        inside = (number >= 0) & (lat >= 0) & (lat < north)
        at_edge = (lon < 0) | (lon >= east)
        place = jnp.where(at_edge, north * east + lat, lat * east + lon)
        return extended[jnp.where(inside, place, north * east + north)]

    copies = []
    for g, group in enumerate(slot_groups):
        span = pl.ds(group.start, len(group))
        for d in range(1, count_az):
            for slot in group:
                outgoing[d - 1, slot] = pick(d, slot)
            device = {"az": lax.rem(az + count_az - d, count_az), "rg": rg}
            copy = remote(
                outgoing.at[d - 1, span],
                incoming.at[d - 1, span],
                block_send.at[g, d - 1],
                block_recv.at[g, d - 1],
                device,
            )
            copy.start()
            copies.append(copy)
    for slot in range(slots):
        table_ref[slot] = pick(0, slot)
    place_columns(anchor_col, hit_ref)
    sums_ref[2] = splat(weight_ref, hit_ref, None)
    near_copies[2].start()
    for load in loads[6:]:
        load.wait()
    first, middle, last = slice(0, rim), slice(rim, lines - rim), slice(lines - rim, lines)
    for g, group in enumerate(slot_groups):
        span = slice(group.start, group.stop)
        total = table_ref[span]
        for d in range(count_az - 1):
            copies[g * (count_az - 1) + d].wait()
            total = total + incoming[d, span]
        table_ref[span] = total
        rows = range(group.start * block[0], group.stop * block[0])
        if g < len(slot_groups) - 1:
            look_up(table_ref, heights_ref, lane_ref, row_ref, slice(0, lines), rows, g == 0)
        else:
            look_up(table_ref, heights_ref, lane_ref, row_ref, first, rows, g == 0)
            look_up(table_ref, heights_ref, lane_ref, row_ref, last, rows, g == 0)
    for part in (first, last):
        flatten_lines(image_ref, factor_ref, heights_ref, flat_ref, part)
    beside = pl.ds(pl.multiple_of((1 - rg) * (samples - LANES), LANES), LANES)
    first_ds, last_ds = pl.ds(0, rim), pl.ds(lines - rim, rim)
    above, below = az - 1, az + 1
    up = [
        remote(flat_ref.at[:, first_ds, :], bottom, send.at[1], recv.at[2], {"az": above, "rg": rg}),
        remote(
            flat_ref.at[:, first_ds, beside], bottom_side, send.at[2], recv.at[4], {"az": above, "rg": 1 - rg}
        ),
    ]
    down = [
        remote(flat_ref.at[:, last_ds, :], top, send.at[3], recv.at[1], {"az": below, "rg": rg}),
        remote(
            flat_ref.at[:, last_ds, beside], top_side, send.at[4], recv.at[3], {"az": below, "rg": 1 - rg}
        ),
    ]

    @pl.when(az > 0)
    def _():
        for copy in up:
            copy.start()

    @pl.when(az < count_az - 1)
    def _():
        for copy in down:
            copy.start()

    look_up(table_ref, heights_ref, lane_ref, row_ref, middle, rows, len(slot_groups) == 1)
    flatten_lines(image_ref, factor_ref, heights_ref, flat_ref, middle)
    side_copy = remote(flat_ref.at[:, :, beside], side, send.at[0], recv.at[0], partner)
    side_copy.start()

    def place(target, centre, nearby):
        left = jnp.where(rg == 1, nearby, 0.0)
        right = jnp.where(rg == 0, nearby, 0.0)
        for part in range(2):
            wide = jnp.concatenate([left[part], centre[part], right[part]], axis=1)
            padded_ref[part, target, :] = wide[:, LANES - rim : 2 * LANES - rim + samples]

    side_copy.wait()
    place(slice(rim, rim + lines), flat_ref[...], side[...])

    @pl.when(az > 0)
    def _():
        for copy in up:
            copy.wait_send()

    @pl.when(az < count_az - 1)
    def _():
        for copy in down:
            copy.wait_send()

    @pl.when(az > 0)
    def _():
        for copy in down:
            copy.wait_recv()
        place(slice(0, rim), top[...], top_side[...])

    @pl.when(az == 0)
    def _():
        padded_ref[:, :rim, :] = jnp.zeros((2, rim, padded_ref.shape[2]), F32)

    @pl.when(az < count_az - 1)
    def _():
        for copy in up:
            copy.wait_recv()
        place(slice(rim + lines, 2 * rim + lines), bottom[...], bottom_side[...])

    @pl.when(az == count_az - 1)
    def _():
        padded_ref[:, rim + lines :, :] = jnp.zeros((2, rim, padded_ref.shape[2]), F32)

    spread(2)
    looks = goldstein_looks(padded_ref, tables)
    sums_ref[0] = splat(weight_ref, hit_ref, looks[0])
    near_copies[0].start()
    sums_ref[1] = splat(weight_ref, hit_ref, looks[1])
    near_copies[1].start()
    spread(0)
    spread(1)
    weight = jnp.maximum(gathered(2), 1.0)
    out_ref[0] = gathered(0) / weight
    out_ref[1] = gathered(1) / weight


def body(
    complex_phase_image,
    phase_to_topography_factor,
    terrain_model_heights,
    radar_parcel_listing,
    pixel_terrain_position,
    multilook_receiving_patch,
    multilook_base_point,
    multilook_splat_shares,
):
    count_az = lax.axis_size("az")
    count_rg = lax.axis_size("rg")
    assert count_rg == 2
    north, east, points = terrain_model_heights.shape
    slots = radar_parcel_listing.shape[1]
    az_lines, rg_samples = phase_to_topography_factor.shape
    dma = pltpu.SemaphoreType.DMA
    block = (points // LANES, LANES)
    rim = PATCH // 4
    groups = [range(start, min(start + 3, slots)) for start in range(0, slots, 3)]
    tile = (az_lines, rg_samples)
    map_lat = az_lines // LOOK
    map_lon = rg_samples // LOOK
    chunks = map_lat * map_lon // LANES
    whole_lat, whole_lon = map_lat * count_az, map_lon * count_rg
    operands = [
        radar_parcel_listing,
        terrain_model_heights,
        pixel_terrain_position,
        multilook_receiving_patch.reshape(chunks, LANES),
        multilook_base_point.reshape(chunks, LANES),
        multilook_splat_shares,
        phase_to_topography_factor,
        complex_phase_image,
    ] + [jnp.asarray(table) for table in filter_tables()]
    assert len(operands) == 18
    return pl.pallas_call(
        functools.partial(whole_kernel, count_az, rim, groups),
        out_shape=jax.ShapeDtypeStruct((2, map_lat, map_lon), F32),
        in_specs=[pl.BlockSpec(memory_space=pl.ANY)] * len(operands),
        scratch_shapes=[pltpu.VMEM(x.shape, x.dtype) for x in operands]
        + [
            dma((len(operands),)),
            pltpu.VMEM((north * east + north + 1,) + block, F32),
            pltpu.VMEM((north,) + block, F32),
            pltpu.VMEM((8, LANES), jnp.int32),
            pltpu.VMEM((count_az, 8, LANES), jnp.int32),
            pltpu.SMEM((count_az, 8, LANES), jnp.int32),
            pltpu.VMEM((count_az - 1, slots) + block, F32),
            pltpu.VMEM((count_az - 1, slots) + block, F32),
            pltpu.VMEM((slots,) + block, F32),
            pltpu.VMEM(tile, F32),
            pltpu.VMEM(tile, jnp.int32),
            pltpu.VMEM(tile, jnp.int32),
            pltpu.VMEM((2,) + tile, F32),
            pltpu.VMEM((2, rim, rg_samples), F32),
            pltpu.VMEM((2, rim, rg_samples), F32),
            pltpu.VMEM((2, az_lines, LANES), F32),
            pltpu.VMEM((2, rim, LANES), F32),
            pltpu.VMEM((2, rim, LANES), F32),
            dma((2,)),
            dma((count_az - 1,)),
            dma((count_az - 1,)),
            dma((len(groups), count_az - 1)),
            dma((len(groups), count_az - 1)),
            dma,
            dma((5,)),
            dma((5,)),
            pltpu.VMEM((2, az_lines + 2 * rim, rg_samples + LANES), F32),
            pltpu.VMEM((2, whole_lat, chunks * LANES), F32),
            pltpu.VMEM((chunks * LANES, whole_lon), BF16),
            pltpu.VMEM((3, whole_lat, whole_lon), F32),
            pltpu.VMEM((3, whole_lat, map_lon), F32),
            pltpu.VMEM((3, whole_lat, map_lon), F32),
            pltpu.VMEM((3, count_az - 1, map_lat, map_lon), F32),
            dma((3,)),
            dma((3,)),
            dma((3, count_az - 1)),
            dma((3, count_az - 1)),
        ],
        compiler_params=pltpu.CompilerParams(
            collective_id=0, has_side_effects=True, vmem_limit_bytes=56 * 1024 * 1024
        ),
        name="interferogram_map",
    )(*operands)


def solution(mesh):
    return jax.shard_map(
        body,
        mesh=mesh,
        in_specs=(
            P(None, ("scene", "az"), "rg"),
            P(("scene", "az"), "rg"),
            P(("scene", "az"), "rg", None),
            P(("scene", "az", "rg"), None),
            P(("scene", "az"), "rg"),
            P(("scene", "az", "rg"), None),
            P(("scene", "az", "rg")),
            P(None, ("scene", "az", "rg")),
        ),
        out_specs=P(None, ("scene", "az"), "rg"),
        check_vma=False,
    )
```

```python
import functools
import math

import jax
import jax.numpy as jnp
import numpy as np
from jax import lax
from jax.experimental import pallas as pl
from jax.experimental.pallas import tpu as pltpu
from jax.sharding import PartitionSpec as P

PATCH = 64
LOOK = 4
LANES = 128
EPS = 1e-06
F32 = jnp.float32
BF16 = jnp.bfloat16


def halves(value):
    high = value.astype(BF16)
    return high, (value - high.astype(F32)).astype(BF16)


def filter_tables():
    steps = np.arange(PATCH)
    angle = (steps[:, None] * steps[None, :] % PATCH) * (2.0 * math.pi / PATCH)
    cosine, sine = np.cos(angle), np.sin(angle)
    left = np.block([[cosine, sine], [-sine, cosine]])
    step, wide = PATCH // 2, 4 * PATCH
    right = np.zeros((2 * wide, 2 * wide))
    for p in range(4):
        rows, cols = slice(p * step, p * step + PATCH), slice(p * PATCH, (p + 1) * PATCH)
        rows_im = slice(wide + p * step, wide + p * step + PATCH)
        cols_im = slice(wide + p * PATCH, wide + (p + 1) * PATCH)
        right[rows, cols] = cosine
        right[rows, cols_im] = -sine
        right[rows_im, cols] = sine
        right[rows_im, cols_im] = cosine
    group = np.arange(wide) // PATCH
    same = group[:, None] == group[None, :]
    gap = (np.arange(wide)[:, None] - np.arange(wide)[None, :]) % PATCH
    band = same & ((gap <= 1) | (gap == PATCH - 1))
    cells = PATCH // 2 // LOOK
    places = PATCH // 4 + np.arange(cells * LOOK)
    turn = steps[:, None] * places[None, :] % PATCH * (2.0 * math.pi / PATCH)
    mean_re = np.cos(turn).reshape(PATCH, cells, LOOK).mean(axis=2) / PATCH
    mean_im = np.sin(turn).reshape(PATCH, cells, LOOK).mean(axis=2) / PATCH
    back_left = np.block([[mean_re.T, -mean_im.T], [mean_im.T, mean_re.T]])
    back_right = np.zeros((2 * wide, 8 * cells))
    for p in range(4):
        rows = slice(p * PATCH, (p + 1) * PATCH)
        rows_im = slice(wide + p * PATCH, wide + (p + 1) * PATCH)
        cols = slice(p * cells, (p + 1) * cells)
        cols_im = slice((4 + p) * cells, (5 + p) * cells)
        back_right[rows, cols] = mean_re
        back_right[rows, cols_im] = mean_im
        back_right[rows_im, cols] = -mean_im
        back_right[rows_im, cols_im] = mean_re
    tables = []
    for table in (left, right, back_left, back_right):
        high = table.astype(np.float32).astype(jnp.bfloat16)
        tables += [high, (table - high.astype(np.float64)).astype(jnp.bfloat16)]
    return tables + [band.astype(jnp.bfloat16), same.astype(jnp.bfloat16)]


def sine_cosine(angle):
    turns = jnp.floor(angle * (2.0 / math.pi) + 0.5)
    rest = angle - turns * 1.5703125
    rest = rest - turns * 4.837512969970703e-04
    rest = rest - turns * 7.549789948768648e-08
    square = rest * rest
    sine = ((-1.9515295891e-4 * square + 8.3321608736e-3) * square - 1.6666654611e-1) * square
    sine = sine * rest + rest
    cosine = ((2.443315711809948e-5 * square - 1.388731625493765e-3) * square + 4.166664568298827e-2)
    cosine = cosine * square * square - 0.5 * square + 1.0
    quarter = turns.astype(jnp.int32) & 3
    swap = (quarter & 1) == 1
    sine_out = jnp.where(swap, cosine, sine)
    cosine_out = jnp.where(swap, sine, cosine)
    sine_out = jnp.where(quarter >= 2, -sine_out, sine_out)
    cosine_out = jnp.where((quarter == 1) | (quarter == 2), -cosine_out, cosine_out)
    return sine_out, cosine_out


def stacked(left, right):
    rows = left.shape[0]
    high, low = halves(left)
    both = jnp.dot(jnp.concatenate([high, low], axis=0), right[0], preferred_element_type=F32)
    out = both[:rows] + both[rows:]
    if right[1] is None:
        return out
    return out + jnp.dot(high, right[1], preferred_element_type=F32)


def goldstein_looks(padded, tables):
    left_both = jnp.concatenate([tables[0][...], tables[1][...]], axis=0)
    back_both = jnp.concatenate([tables[4][...], tables[5][...]], axis=0)
    right = (tables[2], tables[3])
    back_right = (tables[6], tables[7])
    band, same = tables[8][...], tables[9][...]
    step, wide = PATCH // 2, 4 * PATCH
    lines, samples = padded.shape[1:]
    block_rows = (lines - step) // step
    groups = (samples - LANES) // LANES

    def table_first(both, value):
        rows = both.shape[0] // 2
        high, low = halves(value)
        first = jnp.dot(both, high, preferred_element_type=F32)
        return first[:rows] + first[rows:] + jnp.dot(both[:rows], low, preferred_element_type=F32)

    columns = []
    for u in range(block_rows):
        strip = jnp.concatenate(
            [padded[0, u * step : u * step + PATCH], padded[1, u * step : u * step + PATCH]], axis=0
        )
        columns.append(table_first(left_both, strip))
    windows = [slice(q * LANES, q * LANES + wide) for q in range(groups)]
    real = jnp.concatenate([c[:PATCH, w] for w in windows for c in columns], axis=0)
    imag = jnp.concatenate([c[PATCH:, w] for w in windows for c in columns], axis=0)
    spectrum = stacked(real, (right[0][:wide], right[1][:wide])) + stacked(
        imag, (right[0][wide:], right[1][wide:])
    )
    spec_re, spec_im = spectrum[:, :wide], spectrum[:, wide:]
    size = jnp.sqrt(spec_re * spec_re + spec_im * spec_im)
    across = stacked(size, (band, None))
    patches = groups * block_rows
    pieces = [slice(p * PATCH, (p + 1) * PATCH) for p in range(patches)]
    column_sums = jnp.concatenate(
        [jnp.sum(size[p], axis=0, keepdims=True) for p in pieces], axis=0
    )
    if patches % 16:
        column_sums = jnp.concatenate(
            [column_sums, jnp.zeros((16 - patches % 16, wide), F32)], axis=0
        )
    total = stacked(column_sums, (same, None))
    scale = (1.0 / 9.0) / (total * (1.0 / PATCH**2) + EPS)
    gains = []
    for p, piece in enumerate(pieces):
        part = across[piece]
        around = part + pltpu.roll(part, 1, 0) + pltpu.roll(part, PATCH - 1, 0)
        gains.append(jnp.sqrt(around * scale[p : p + 1]))
    gain = jnp.concatenate(gains, axis=0)
    rows = stacked(spec_re * gain, (back_right[0][:wide], back_right[1][:wide])) + stacked(
        spec_im * gain, (back_right[0][wide:], back_right[1][wide:])
    )
    half = rows.shape[1] // 2
    looks = []
    for u in range(block_rows):
        parts = [rows[pieces[q * block_rows + u]] for q in range(groups)]
        value = jnp.concatenate(
            [
                jnp.concatenate([x[:, :half] for x in parts], axis=1),
                jnp.concatenate([x[:, half:] for x in parts], axis=1),
            ],
            axis=0,
        )
        looks.append(table_first(back_both, value))
    half = looks[0].shape[0] // 2
    return [jnp.concatenate([x[:half] for x in looks], axis=0), jnp.concatenate([x[half:] for x in looks], axis=0)]


def anchors(owner, base, tile_lat, tile_lon, count_rg):
    row = owner // count_rg * tile_lat + base // tile_lon
    return row, owner % count_rg * tile_lon + base % tile_lon


def place_rows(anchor_row, share_ref, row_ref):
    row_ids = lax.broadcasted_iota(jnp.int32, (row_ref.shape[1], LANES), 0)
    for i in range(anchor_row.shape[0]):
        span = slice(i * LANES, (i + 1) * LANES)
        gap = row_ids - anchor_row[i : i + 1]
        for c in range(2):
            upper, lower = share_ref[c : c + 1, span], share_ref[2 + c : 3 + c, span]
            row_ref[c, :, span] = jnp.where(gap == 0, upper, jnp.where(gap == 1, lower, 0.0))


def place_columns(anchor_col, hit_ref):
    col_ids = lax.broadcasted_iota(jnp.int32, (LANES, hit_ref.shape[1]), 1).astype(F32)
    for i in range(anchor_col.shape[0]):
        column = jnp.broadcast_to(anchor_col[i : i + 1].astype(F32), (LANES, LANES)).T
        column = jnp.concatenate([column] * (hit_ref.shape[1] // LANES), axis=1)
        hit_ref[i * LANES : (i + 1) * LANES, :] = jnp.where(column == col_ids, 1.0, 0.0).astype(BF16)


def splat(row_ref, hit_ref, look):
    chunks = hit_ref.shape[0] // LANES
    rows = row_ref.shape[1]
    values = []
    for c in range(2):
        if look is None:
            value = row_ref[c]
        else:
            value = jnp.concatenate(
                [row_ref[c, :, i * LANES : (i + 1) * LANES] * look[i : i + 1] for i in range(chunks)],
                axis=1,
            )
        values += halves(value)
    sums = jnp.dot(jnp.concatenate(values, axis=0), hit_ref[...], preferred_element_type=F32)
    moved = pltpu.roll(sums[2 * rows : 3 * rows] + sums[3 * rows :], 1, 1)
    first = lax.broadcasted_iota(jnp.int32, moved.shape, 1) == 0
    return sums[:rows] + sums[rows : 2 * rows] + jnp.where(first, 0.0, moved)


MESH = pl.DeviceIdType.MESH


def peers(count_az):
    az, rg = lax.axis_index("az"), lax.axis_index("rg")
    others = [{"az": lax.rem(az + d, count_az), "rg": rg} for d in range(1, count_az)]
    return az, rg, others, {"az": az, "rg": 1 - rg}


def greet(devices):
    barrier = pltpu.get_barrier_semaphore()
    for device in devices:
        pl.semaphore_signal(barrier, inc=1, device_id=device, device_id_type=MESH)
    pl.semaphore_wait(barrier, len(devices))


def remote(source, target, send_sem, recv_sem, device):
    return pltpu.make_async_remote_copy(
        src_ref=source,
        dst_ref=target,
        send_sem=send_sem,
        recv_sem=recv_sem,
        device_id=device,
        device_id_type=MESH,
    )


def spread_rows(table_ref, wide_ref, rows):
    for r in rows:
        wide_ref[r] = jnp.broadcast_to(table_ref[r // 8, r % 8 : r % 8 + 1, :], wide_ref.shape[1:])


def look_up(wide_ref, heights_ref, lane_ref, row_ref, pieces, rows, fresh):
    def one_column(column, carry):
        span = pl.ds(pl.multiple_of(column * LANES, LANES), LANES)
        lane = jnp.concatenate([lane_ref[piece, span] for piece in pieces], axis=0)
        row = jnp.concatenate([row_ref[piece, span] for piece in pieces], axis=0)
        if fresh:
            heights = jnp.zeros(lane.shape, F32)
        else:
            heights = jnp.concatenate([heights_ref[piece, span] for piece in pieces], axis=0)
        for r in rows:
            source = jnp.concatenate([wide_ref[r]] * (lane.shape[0] // wide_ref.shape[1]), axis=0)
            picked = jnp.take_along_axis(source, lane, axis=1, mode="promise_in_bounds")
            heights = jnp.where(row == r, picked, heights)
        start = 0
        for piece in pieces:
            count = piece.stop - piece.start
            heights_ref[piece, span] = heights[start : start + count]
            start += count
        return carry

    lax.fori_loop(0, heights_ref.shape[1] // LANES, one_column, 0)


def flatten_lines(image_ref, factor_ref, heights_ref, flat_ref, lines):
    sine, cosine = sine_cosine(factor_ref[lines, :] * heights_ref[lines, :])
    real, imag = image_ref[0, lines, :], image_ref[1, lines, :]
    flat_ref[0, lines, :] = real * cosine + imag * sine
    flat_ref[1, lines, :] = imag * cosine - real * sine


def whole_kernel(
    count_az,
    rim,
    slot_groups,
    *refs,
):
    sources, refs = refs[:18], refs[18:]
    out_ref, refs = refs[0], refs[1:]
    held, refs = refs[:18], refs[18:]
    list_ref, terrain_ref, position_ref, owner_ref, base_ref, share_ref, factor_ref, image_ref = held[:8]
    tables = held[8:]
    (
        load_sems,
        extended,
        edge,
        own_list,
        lists,
        lists_smem,
        outgoing,
        incoming,
        table_ref,
        wide_ref,
        heights_ref,
        lane_ref,
        row_ref,
        flat_ref,
        top,
        bottom,
        side,
        top_side,
        bottom_side,
        edge_sems,
        list_send,
        list_recv,
        block_send,
        block_recv,
        local_sem,
        send,
        recv,
        padded_ref,
        weight_ref,
        hit_ref,
        sums_ref,
        half,
        near,
        far,
        near_send,
        near_recv,
        far_send,
        far_recv,
    ) = refs
    north, east = terrain_ref.shape[:2]
    slots = list_ref.shape[1]
    block = extended.shape[1:]
    lines, samples = factor_ref.shape
    az, rg, others, partner = peers(count_az)
    barrier = pltpu.get_barrier_semaphore()
    crossed = [
        {"az": lax.rem(az + d, count_az), "rg": 1 - rg} for d in (1, count_az - 1)
    ]
    greeted = others + [partner] + crossed
    loads = [
        pltpu.make_async_copy(source, target, load_sems.at[n])
        for n, (source, target) in enumerate(zip(sources, held))
    ]
    for load in loads[:2]:
        load.start()
    for device in greeted:
        pl.semaphore_signal(barrier, inc=1, device_id=device, device_id_type=MESH)
    for load in loads[2:8]:
        load.start()
    loads[0].wait()
    own_list[...] = jnp.full(own_list.shape, -1, jnp.int32)
    own_list[0:1, 0:slots] = list_ref[...]
    lists[0] = own_list[...]
    loads[1].wait()
    for lat in range(north):
        extended[lat * east : (lat + 1) * east] = terrain_ref[lat].reshape((east,) + block)
    extended[north * east + north] = jnp.zeros(block, F32)
    for lat in range(north):
        edge[lat] = jnp.where(rg == 0, extended[lat * east + east - 1], extended[lat * east])
    pl.semaphore_wait(barrier, len(greeted))
    list_copies = [
        remote(own_list, lists.at[d + 1], list_send.at[d], list_recv.at[d], device)
        for d, device in enumerate(others)
    ]
    for copy in list_copies:
        copy.start()
    edge_copy = remote(
        edge, extended.at[pl.ds(north * east, north)], edge_sems.at[0], edge_sems.at[1], partner
    )
    edge_copy.start()
    for load in loads[8:]:
        load.start()
    channels, map_lat, map_lon = sums_ref.shape
    tile, lanes = out_ref.shape[1:]
    mine = pl.ds(pl.multiple_of(rg * lanes, LANES), lanes)
    theirs = pl.ds(pl.multiple_of((1 - rg) * lanes, LANES), lanes)
    near_copies = [
        remote(sums_ref.at[c, :, theirs], near.at[c], near_send.at[c], near_recv.at[c], partner)
        for c in range(channels)
    ]
    far_copies = [
        [
            remote(
                half.at[c, pl.ds(pl.multiple_of(device["az"] * tile, 8), tile), :],
                far.at[c, d],
                far_send.at[c, d],
                far_recv.at[c, d],
                device,
            )
            for d, device in enumerate(others)
        ]
        for c in range(channels)
    ]

    def spread(c):
        near_copies[c].wait()
        half[c] = sums_ref[c, :, mine] + near[c]
        for copy in far_copies[c]:
            copy.start()

    def gathered(c):
        total = half[c, pl.ds(pl.multiple_of(az * tile, 8), tile), :]
        for d, copy in enumerate(far_copies[c]):
            copy.wait()
            total = total + far[c, d]
        return total

    loads[2].wait()
    position = position_ref[...]
    lane_ref[...] = position & (LANES - 1)
    row_ref[...] = lax.shift_right_logical(position, LANES.bit_length() - 1)
    for n in range(3, 6):
        loads[n].wait()
    anchor_row, anchor_col = anchors(owner_ref[...], base_ref[...], tile, lanes, map_lon // lanes)
    place_rows(anchor_row, share_ref, weight_ref)
    for copy in list_copies:
        copy.wait()
    to_smem = pltpu.make_async_copy(lists, lists_smem, local_sem)
    to_smem.start()
    edge_copy.wait()
    to_smem.wait()

    def pick(d, slot):
        number = lists_smem[d, 0, slot]
        lat = number // (2 * east) - az * north
        lon = number % (2 * east) - rg * east
        inside = (number >= 0) & (lat >= 0) & (lat < north)
        at_edge = (lon < 0) | (lon >= east)
        place = jnp.where(at_edge, north * east + lat, lat * east + lon)
        return extended[jnp.where(inside, place, north * east + north)]

    copies = []
    for g, group in enumerate(slot_groups):
        span = pl.ds(group.start, len(group))
        for d in range(1, count_az):
            for slot in group:
                outgoing[d - 1, slot] = pick(d, slot)
            device = {"az": lax.rem(az + count_az - d, count_az), "rg": rg}
            copy = remote(
                outgoing.at[d - 1, span],
                incoming.at[d - 1, span],
                block_send.at[g, d - 1],
                block_recv.at[g, d - 1],
                device,
            )
            copy.start()
            copies.append(copy)
    for slot in range(slots):
        table_ref[slot] = pick(0, slot)
    place_columns(anchor_col, hit_ref)
    sums_ref[2] = splat(weight_ref, hit_ref, None)
    near_copies[2].start()
    for load in loads[6:]:
        load.wait()
    first, middle, last = slice(0, rim), slice(rim, lines - rim), slice(lines - rim, lines)
    for g, group in enumerate(slot_groups):
        span = slice(group.start, group.stop)
        total = table_ref[span]
        for d in range(count_az - 1):
            copies[g * (count_az - 1) + d].wait()
            total = total + incoming[d, span]
        table_ref[span] = total
        rows = range(group.start * block[0], group.stop * block[0])
        spread_rows(table_ref, wide_ref, rows)
        look_up(wide_ref, heights_ref, lane_ref, row_ref, (first, last), rows, g == 0)
    for part in (first, last):
        flatten_lines(image_ref, factor_ref, heights_ref, flat_ref, part)
    beside = pl.ds(pl.multiple_of((1 - rg) * (samples - LANES), LANES), LANES)
    first_ds, last_ds = pl.ds(0, rim), pl.ds(lines - rim, rim)
    above, below = az - 1, az + 1
    up = [
        remote(flat_ref.at[:, first_ds, :], bottom, send.at[1], recv.at[2], {"az": above, "rg": rg}),
        remote(
            flat_ref.at[:, first_ds, beside], bottom_side, send.at[2], recv.at[4], {"az": above, "rg": 1 - rg}
        ),
    ]
    down = [
        remote(flat_ref.at[:, last_ds, :], top, send.at[3], recv.at[1], {"az": below, "rg": rg}),
        remote(
            flat_ref.at[:, last_ds, beside], top_side, send.at[4], recv.at[3], {"az": below, "rg": 1 - rg}
        ),
    ]

    @pl.when(az > 0)
    def _():
        for copy in up:
            copy.start()

    @pl.when(az < count_az - 1)
    def _():
        for copy in down:
            copy.start()

    look_up(wide_ref, heights_ref, lane_ref, row_ref, (middle,), range(slots * block[0]), True)
    flatten_lines(image_ref, factor_ref, heights_ref, flat_ref, middle)
    side_copy = remote(flat_ref.at[:, :, beside], side, send.at[0], recv.at[0], partner)
    side_copy.start()

    def place(target, centre, nearby):
        left = jnp.where(rg == 1, nearby, 0.0)
        right = jnp.where(rg == 0, nearby, 0.0)
        for part in range(2):
            wide = jnp.concatenate([left[part], centre[part], right[part]], axis=1)
            padded_ref[part, target, :] = wide[:, LANES - rim : 2 * LANES - rim + samples]

    side_copy.wait()
    place(slice(rim, rim + lines), flat_ref[...], side[...])

    @pl.when(az > 0)
    def _():
        for copy in up:
            copy.wait_send()

    @pl.when(az < count_az - 1)
    def _():
        for copy in down:
            copy.wait_send()

    @pl.when(az > 0)
    def _():
        for copy in down:
            copy.wait_recv()
        place(slice(0, rim), top[...], top_side[...])

    @pl.when(az == 0)
    def _():
        padded_ref[:, :rim, :] = jnp.zeros((2, rim, padded_ref.shape[2]), F32)

    @pl.when(az < count_az - 1)
    def _():
        for copy in up:
            copy.wait_recv()
        place(slice(rim + lines, 2 * rim + lines), bottom[...], bottom_side[...])

    @pl.when(az == count_az - 1)
    def _():
        padded_ref[:, rim + lines :, :] = jnp.zeros((2, rim, padded_ref.shape[2]), F32)

    spread(2)
    looks = goldstein_looks(padded_ref, tables)
    sums_ref[0] = splat(weight_ref, hit_ref, looks[0])
    near_copies[0].start()
    sums_ref[1] = splat(weight_ref, hit_ref, looks[1])
    near_copies[1].start()
    spread(0)
    spread(1)
    weight = jnp.maximum(gathered(2), 1.0)
    out_ref[0] = gathered(0) / weight
    out_ref[1] = gathered(1) / weight


def body(
    complex_phase_image,
    phase_to_topography_factor,
    terrain_model_heights,
    radar_parcel_listing,
    pixel_terrain_position,
    multilook_receiving_patch,
    multilook_base_point,
    multilook_splat_shares,
):
    count_az = lax.axis_size("az")
    count_rg = lax.axis_size("rg")
    assert count_rg == 2
    north, east, points = terrain_model_heights.shape
    slots = radar_parcel_listing.shape[1]
    az_lines, rg_samples = phase_to_topography_factor.shape
    dma = pltpu.SemaphoreType.DMA
    block = (points // LANES, LANES)
    rim = PATCH // 4
    groups = [range(start, min(start + 3, slots)) for start in range(0, slots, 3)]
    tile = (az_lines, rg_samples)
    map_lat = az_lines // LOOK
    map_lon = rg_samples // LOOK
    chunks = map_lat * map_lon // LANES
    whole_lat, whole_lon = map_lat * count_az, map_lon * count_rg
    operands = [
        radar_parcel_listing,
        terrain_model_heights,
        pixel_terrain_position,
        multilook_receiving_patch.reshape(chunks, LANES),
        multilook_base_point.reshape(chunks, LANES),
        multilook_splat_shares,
        phase_to_topography_factor,
        complex_phase_image,
    ] + [jnp.asarray(table) for table in filter_tables()]
    assert len(operands) == 18
    return pl.pallas_call(
        functools.partial(whole_kernel, count_az, rim, groups),
        out_shape=jax.ShapeDtypeStruct((2, map_lat, map_lon), F32),
        in_specs=[pl.BlockSpec(memory_space=pl.ANY)] * len(operands),
        scratch_shapes=[pltpu.VMEM(x.shape, x.dtype) for x in operands]
        + [
            dma((len(operands),)),
            pltpu.VMEM((north * east + north + 1,) + block, F32),
            pltpu.VMEM((north,) + block, F32),
            pltpu.VMEM((8, LANES), jnp.int32),
            pltpu.VMEM((count_az, 8, LANES), jnp.int32),
            pltpu.SMEM((count_az, 8, LANES), jnp.int32),
            pltpu.VMEM((count_az - 1, slots) + block, F32),
            pltpu.VMEM((count_az - 1, slots) + block, F32),
            pltpu.VMEM((slots,) + block, F32),
            pltpu.VMEM((slots * block[0], 8, LANES), F32),
            pltpu.VMEM(tile, F32),
            pltpu.VMEM(tile, jnp.int32),
            pltpu.VMEM(tile, jnp.int32),
            pltpu.VMEM((2,) + tile, F32),
            pltpu.VMEM((2, rim, rg_samples), F32),
            pltpu.VMEM((2, rim, rg_samples), F32),
            pltpu.VMEM((2, az_lines, LANES), F32),
            pltpu.VMEM((2, rim, LANES), F32),
            pltpu.VMEM((2, rim, LANES), F32),
            dma((2,)),
            dma((count_az - 1,)),
            dma((count_az - 1,)),
            dma((len(groups), count_az - 1)),
            dma((len(groups), count_az - 1)),
            dma,
            dma((5,)),
            dma((5,)),
            pltpu.VMEM((2, az_lines + 2 * rim, rg_samples + LANES), F32),
            pltpu.VMEM((2, whole_lat, chunks * LANES), F32),
            pltpu.VMEM((chunks * LANES, whole_lon), BF16),
            pltpu.VMEM((3, whole_lat, whole_lon), F32),
            pltpu.VMEM((3, whole_lat, map_lon), F32),
            pltpu.VMEM((3, whole_lat, map_lon), F32),
            pltpu.VMEM((3, count_az - 1, map_lat, map_lon), F32),
            dma((3,)),
            dma((3,)),
            dma((3, count_az - 1)),
            dma((3, count_az - 1)),
        ],
        compiler_params=pltpu.CompilerParams(
            collective_id=0, has_side_effects=True, vmem_limit_bytes=56 * 1024 * 1024
        ),
        name="interferogram_map",
    )(*operands)


def solution(mesh):
    return jax.shard_map(
        body,
        mesh=mesh,
        in_specs=(
            P(None, ("scene", "az"), "rg"),
            P(("scene", "az"), "rg"),
            P(("scene", "az"), "rg", None),
            P(("scene", "az", "rg"), None),
            P(("scene", "az"), "rg"),
            P(("scene", "az", "rg"), None),
            P(("scene", "az", "rg")),
            P(None, ("scene", "az", "rg")),
        ),
        out_specs=P(None, ("scene", "az"), "rg"),
        check_vma=False,
    )
```

```python
import functools
import math

import jax
import jax.numpy as jnp
import numpy as np
from jax import lax
from jax.experimental import pallas as pl
from jax.experimental.pallas import tpu as pltpu
from jax.sharding import PartitionSpec as P

PATCH = 64
LOOK = 4
LANES = 128
EPS = 1e-06
F32 = jnp.float32
BF16 = jnp.bfloat16


def halves(value):
    high = value.astype(BF16)
    return high, (value - high.astype(F32)).astype(BF16)


def filter_tables():
    steps = np.arange(PATCH)
    angle = (steps[:, None] * steps[None, :] % PATCH) * (2.0 * math.pi / PATCH)
    cosine, sine = np.cos(angle), np.sin(angle)
    left = np.block([[cosine, sine], [-sine, cosine]])
    step, wide = PATCH // 2, 4 * PATCH
    right = np.zeros((2 * wide, 2 * wide))
    for p in range(4):
        rows, cols = slice(p * step, p * step + PATCH), slice(p * PATCH, (p + 1) * PATCH)
        rows_im = slice(wide + p * step, wide + p * step + PATCH)
        cols_im = slice(wide + p * PATCH, wide + (p + 1) * PATCH)
        right[rows, cols] = cosine
        right[rows, cols_im] = -sine
        right[rows_im, cols] = sine
        right[rows_im, cols_im] = cosine
    group = np.arange(wide) // PATCH
    same = group[:, None] == group[None, :]
    gap = (np.arange(wide)[:, None] - np.arange(wide)[None, :]) % PATCH
    band = same & ((gap <= 1) | (gap == PATCH - 1))
    cells = PATCH // 2 // LOOK
    places = PATCH // 4 + np.arange(cells * LOOK)
    turn = steps[:, None] * places[None, :] % PATCH * (2.0 * math.pi / PATCH)
    mean_re = np.cos(turn).reshape(PATCH, cells, LOOK).mean(axis=2) / PATCH
    mean_im = np.sin(turn).reshape(PATCH, cells, LOOK).mean(axis=2) / PATCH
    back_left = np.block([[mean_re.T, -mean_im.T], [mean_im.T, mean_re.T]])
    back_right = np.zeros((2 * wide, 8 * cells))
    for p in range(4):
        rows = slice(p * PATCH, (p + 1) * PATCH)
        rows_im = slice(wide + p * PATCH, wide + (p + 1) * PATCH)
        cols = slice(p * cells, (p + 1) * cells)
        cols_im = slice((4 + p) * cells, (5 + p) * cells)
        back_right[rows, cols] = mean_re
        back_right[rows, cols_im] = mean_im
        back_right[rows_im, cols] = -mean_im
        back_right[rows_im, cols_im] = mean_re
    tables = []
    for table in (left, right, back_left, back_right):
        high = table.astype(np.float32).astype(jnp.bfloat16)
        tables += [high, (table - high.astype(np.float64)).astype(jnp.bfloat16)]
    return tables + [band.astype(jnp.bfloat16), same.astype(jnp.bfloat16)]


def sine_cosine(angle):
    turns = jnp.floor(angle * (2.0 / math.pi) + 0.5)
    rest = angle - turns * 1.5703125
    rest = rest - turns * 4.837512969970703e-04
    rest = rest - turns * 7.549789948768648e-08
    square = rest * rest
    sine = ((-1.9515295891e-4 * square + 8.3321608736e-3) * square - 1.6666654611e-1) * square
    sine = sine * rest + rest
    cosine = ((2.443315711809948e-5 * square - 1.388731625493765e-3) * square + 4.166664568298827e-2)
    cosine = cosine * square * square - 0.5 * square + 1.0
    quarter = turns.astype(jnp.int32) & 3
    swap = (quarter & 1) == 1
    sine_out = jnp.where(swap, cosine, sine)
    cosine_out = jnp.where(swap, sine, cosine)
    sine_out = jnp.where(quarter >= 2, -sine_out, sine_out)
    cosine_out = jnp.where((quarter == 1) | (quarter == 2), -cosine_out, cosine_out)
    return sine_out, cosine_out


def stacked(left, right):
    rows = left.shape[0]
    high, low = halves(left)
    both = jnp.dot(jnp.concatenate([high, low], axis=0), right[0], preferred_element_type=F32)
    out = both[:rows] + both[rows:]
    if right[1] is None:
        return out
    return out + jnp.dot(high, right[1], preferred_element_type=F32)


def goldstein_looks(padded, tables):
    left_both = jnp.concatenate([tables[0][...], tables[1][...]], axis=0)
    back_both = jnp.concatenate([tables[4][...], tables[5][...]], axis=0)
    right = (tables[2], tables[3])
    back_right = (tables[6], tables[7])
    band, same = tables[8][...], tables[9][...]
    step, wide = PATCH // 2, 4 * PATCH
    lines, samples = padded.shape[1:]
    block_rows = (lines - step) // step
    groups = (samples - LANES) // LANES

    def table_first(both, value):
        rows = both.shape[0] // 2
        high, low = halves(value)
        first = jnp.dot(both, high, preferred_element_type=F32)
        return first[:rows] + first[rows:] + jnp.dot(both[:rows], low, preferred_element_type=F32)

    columns = []
    for u in range(block_rows):
        strip = jnp.concatenate(
            [padded[0, u * step : u * step + PATCH], padded[1, u * step : u * step + PATCH]], axis=0
        )
        columns.append(table_first(left_both, strip))
    windows = [slice(q * LANES, q * LANES + wide) for q in range(groups)]
    real = jnp.concatenate([c[:PATCH, w] for w in windows for c in columns], axis=0)
    imag = jnp.concatenate([c[PATCH:, w] for w in windows for c in columns], axis=0)
    spectrum = stacked(real, (right[0][:wide], right[1][:wide])) + stacked(
        imag, (right[0][wide:], right[1][wide:])
    )
    spec_re, spec_im = spectrum[:, :wide], spectrum[:, wide:]
    size = jnp.sqrt(spec_re * spec_re + spec_im * spec_im)
    across = stacked(size, (band, None))
    patches = groups * block_rows
    pieces = [slice(p * PATCH, (p + 1) * PATCH) for p in range(patches)]
    column_sums = jnp.concatenate(
        [jnp.sum(size[p], axis=0, keepdims=True) for p in pieces], axis=0
    )
    if patches % 16:
        column_sums = jnp.concatenate(
            [column_sums, jnp.zeros((16 - patches % 16, wide), F32)], axis=0
        )
    total = stacked(column_sums, (same, None))
    scale = (1.0 / 9.0) / (total * (1.0 / PATCH**2) + EPS)
    gains = []
    for p, piece in enumerate(pieces):
        part = across[piece]
        around = part + pltpu.roll(part, 1, 0) + pltpu.roll(part, PATCH - 1, 0)
        gains.append(jnp.sqrt(around * scale[p : p + 1]))
    gain = jnp.concatenate(gains, axis=0)
    rows = stacked(spec_re * gain, (back_right[0][:wide], back_right[1][:wide])) + stacked(
        spec_im * gain, (back_right[0][wide:], back_right[1][wide:])
    )
    half = rows.shape[1] // 2
    looks = []
    for u in range(block_rows):
        parts = [rows[pieces[q * block_rows + u]] for q in range(groups)]
        value = jnp.concatenate(
            [
                jnp.concatenate([x[:, :half] for x in parts], axis=1),
                jnp.concatenate([x[:, half:] for x in parts], axis=1),
            ],
            axis=0,
        )
        looks.append(table_first(back_both, value))
    half = looks[0].shape[0] // 2
    return [jnp.concatenate([x[:half] for x in looks], axis=0), jnp.concatenate([x[half:] for x in looks], axis=0)]


def anchors(owner, base, tile_lat, tile_lon, count_rg):
    row = owner // count_rg * tile_lat + base // tile_lon
    return row, owner % count_rg * tile_lon + base % tile_lon


def place_rows(anchor_row, share_ref, row_ref):
    row_ids = lax.broadcasted_iota(jnp.int32, (row_ref.shape[1], LANES), 0)
    for i in range(anchor_row.shape[0]):
        span = slice(i * LANES, (i + 1) * LANES)
        gap = row_ids - anchor_row[i : i + 1]
        for c in range(2):
            upper, lower = share_ref[c : c + 1, span], share_ref[2 + c : 3 + c, span]
            row_ref[c, :, span] = jnp.where(gap == 0, upper, jnp.where(gap == 1, lower, 0.0))


def place_columns(anchor_col, hit_ref):
    col_ids = lax.broadcasted_iota(jnp.int32, (LANES, hit_ref.shape[1]), 1).astype(F32)
    for i in range(anchor_col.shape[0]):
        column = jnp.broadcast_to(anchor_col[i : i + 1].astype(F32), (LANES, LANES)).T
        column = jnp.concatenate([column] * (hit_ref.shape[1] // LANES), axis=1)
        hit_ref[i * LANES : (i + 1) * LANES, :] = jnp.where(column == col_ids, 1.0, 0.0).astype(BF16)


def splat(row_ref, hit_ref, look):
    chunks = hit_ref.shape[0] // LANES
    rows = row_ref.shape[1]
    values = []
    for c in range(2):
        if look is None:
            value = row_ref[c]
        else:
            value = jnp.concatenate(
                [row_ref[c, :, i * LANES : (i + 1) * LANES] * look[i : i + 1] for i in range(chunks)],
                axis=1,
            )
        values += halves(value)
    sums = jnp.dot(jnp.concatenate(values, axis=0), hit_ref[...], preferred_element_type=F32)
    moved = pltpu.roll(sums[2 * rows : 3 * rows] + sums[3 * rows :], 1, 1)
    first = lax.broadcasted_iota(jnp.int32, moved.shape, 1) == 0
    return sums[:rows] + sums[rows : 2 * rows] + jnp.where(first, 0.0, moved)


MESH = pl.DeviceIdType.MESH


def peers(count_az):
    az, rg = lax.axis_index("az"), lax.axis_index("rg")
    others = [{"az": lax.rem(az + d, count_az), "rg": rg} for d in range(1, count_az)]
    return az, rg, others, {"az": az, "rg": 1 - rg}


def greet(devices):
    barrier = pltpu.get_barrier_semaphore()
    for device in devices:
        pl.semaphore_signal(barrier, inc=1, device_id=device, device_id_type=MESH)
    pl.semaphore_wait(barrier, len(devices))


def remote(source, target, send_sem, recv_sem, device):
    return pltpu.make_async_remote_copy(
        src_ref=source,
        dst_ref=target,
        send_sem=send_sem,
        recv_sem=recv_sem,
        device_id=device,
        device_id_type=MESH,
    )


def spread_rows(table_ref, wide_ref, rows):
    for r in rows:
        wide_ref[r] = jnp.broadcast_to(table_ref[r // 8, r % 8 : r % 8 + 1, :], wide_ref.shape[1:])


def look_up(wide_ref, heights_ref, lane_ref, row_ref, pieces, rows, fresh, columns, after=None):
    first, start_at, stop_at = columns
    count_columns = heights_ref.shape[1] // LANES

    def one_column(step, carry):
        column = lax.rem(first + step, count_columns)
        span = pl.ds(pl.multiple_of(column * LANES, LANES), LANES)
        lane = jnp.concatenate([lane_ref[piece, span] for piece in pieces], axis=0)
        row = jnp.concatenate([row_ref[piece, span] for piece in pieces], axis=0)
        if fresh:
            heights = jnp.zeros(lane.shape, F32)
        else:
            heights = jnp.concatenate([heights_ref[piece, span] for piece in pieces], axis=0)
        for r in rows:
            source = jnp.concatenate([wide_ref[r]] * (lane.shape[0] // wide_ref.shape[1]), axis=0)
            picked = jnp.take_along_axis(source, lane, axis=1, mode="promise_in_bounds")
            heights = jnp.where(row == r, picked, heights)
        start = 0
        for piece in pieces:
            count = piece.stop - piece.start
            heights_ref[piece, span] = heights[start : start + count]
            start += count
        if after is not None:
            after(span)
        return carry

    lax.fori_loop(start_at, stop_at, one_column, 0)


def flatten_lines(image_ref, factor_ref, heights_ref, flat_ref, lines, span):
    sine, cosine = sine_cosine(factor_ref[lines, span] * heights_ref[lines, span])
    real, imag = image_ref[0, lines, span], image_ref[1, lines, span]
    flat_ref[0, lines, span] = real * cosine + imag * sine
    flat_ref[1, lines, span] = imag * cosine - real * sine


def whole_kernel(
    count_az,
    rim,
    slot_groups,
    *refs,
):
    sources, refs = refs[:18], refs[18:]
    out_ref, refs = refs[0], refs[1:]
    held, refs = refs[:18], refs[18:]
    list_ref, terrain_ref, position_ref, owner_ref, base_ref, share_ref, factor_ref, image_ref = held[:8]
    tables = held[8:]
    (
        load_sems,
        extended,
        edge,
        own_list,
        lists,
        lists_smem,
        outgoing,
        incoming,
        table_ref,
        wide_ref,
        heights_ref,
        lane_ref,
        row_ref,
        flat_ref,
        top,
        bottom,
        side,
        top_side,
        bottom_side,
        edge_sems,
        list_send,
        list_recv,
        block_send,
        block_recv,
        local_sem,
        send,
        recv,
        padded_ref,
        weight_ref,
        hit_ref,
        sums_ref,
        half,
        near,
        far,
        near_send,
        near_recv,
        far_send,
        far_recv,
    ) = refs
    north, east = terrain_ref.shape[:2]
    slots = list_ref.shape[1]
    block = extended.shape[1:]
    lines, samples = factor_ref.shape
    az, rg, others, partner = peers(count_az)
    barrier = pltpu.get_barrier_semaphore()
    crossed = [
        {"az": lax.rem(az + d, count_az), "rg": 1 - rg} for d in (1, count_az - 1)
    ]
    greeted = others + [partner] + crossed
    loads = [
        pltpu.make_async_copy(source, target, load_sems.at[n])
        for n, (source, target) in enumerate(zip(sources, held))
    ]
    for load in loads[:2]:
        load.start()
    for device in greeted:
        pl.semaphore_signal(barrier, inc=1, device_id=device, device_id_type=MESH)
    for load in loads[2:8]:
        load.start()
    loads[0].wait()
    own_list[...] = jnp.full(own_list.shape, -1, jnp.int32)
    own_list[0:1, 0:slots] = list_ref[...]
    lists[0] = own_list[...]
    loads[1].wait()
    for lat in range(north):
        extended[lat * east : (lat + 1) * east] = terrain_ref[lat].reshape((east,) + block)
    extended[north * east + north] = jnp.zeros(block, F32)
    for lat in range(north):
        edge[lat] = jnp.where(rg == 0, extended[lat * east + east - 1], extended[lat * east])
    pl.semaphore_wait(barrier, len(greeted))
    list_copies = [
        remote(own_list, lists.at[d + 1], list_send.at[d], list_recv.at[d], device)
        for d, device in enumerate(others)
    ]
    for copy in list_copies:
        copy.start()
    edge_copy = remote(
        edge, extended.at[pl.ds(north * east, north)], edge_sems.at[0], edge_sems.at[1], partner
    )
    edge_copy.start()
    for load in loads[8:]:
        load.start()
    channels, map_lat, map_lon = sums_ref.shape
    tile, lanes = out_ref.shape[1:]
    mine = pl.ds(pl.multiple_of(rg * lanes, LANES), lanes)
    theirs = pl.ds(pl.multiple_of((1 - rg) * lanes, LANES), lanes)
    near_copies = [
        remote(sums_ref.at[c, :, theirs], near.at[c], near_send.at[c], near_recv.at[c], partner)
        for c in range(channels)
    ]
    far_copies = [
        [
            remote(
                half.at[c, pl.ds(pl.multiple_of(device["az"] * tile, 8), tile), :],
                far.at[c, d],
                far_send.at[c, d],
                far_recv.at[c, d],
                device,
            )
            for d, device in enumerate(others)
        ]
        for c in range(channels)
    ]

    def spread(c):
        near_copies[c].wait()
        half[c] = sums_ref[c, :, mine] + near[c]
        for copy in far_copies[c]:
            copy.start()

    def gathered(c):
        total = half[c, pl.ds(pl.multiple_of(az * tile, 8), tile), :]
        for d, copy in enumerate(far_copies[c]):
            copy.wait()
            total = total + far[c, d]
        return total

    loads[2].wait()
    position = position_ref[...]
    lane_ref[...] = position & (LANES - 1)
    row_ref[...] = lax.shift_right_logical(position, LANES.bit_length() - 1)
    for n in range(3, 6):
        loads[n].wait()
    anchor_row, anchor_col = anchors(owner_ref[...], base_ref[...], tile, lanes, map_lon // lanes)
    place_rows(anchor_row, share_ref, weight_ref)
    for copy in list_copies:
        copy.wait()
    to_smem = pltpu.make_async_copy(lists, lists_smem, local_sem)
    to_smem.start()
    edge_copy.wait()
    to_smem.wait()

    def pick(d, slot):
        number = lists_smem[d, 0, slot]
        lat = number // (2 * east) - az * north
        lon = number % (2 * east) - rg * east
        inside = (number >= 0) & (lat >= 0) & (lat < north)
        at_edge = (lon < 0) | (lon >= east)
        place = jnp.where(at_edge, north * east + lat, lat * east + lon)
        return extended[jnp.where(inside, place, north * east + north)]

    copies = []
    for g, group in enumerate(slot_groups):
        span = pl.ds(group.start, len(group))
        for d in range(1, count_az):
            for slot in group:
                outgoing[d - 1, slot] = pick(d, slot)
            device = {"az": lax.rem(az + count_az - d, count_az), "rg": rg}
            copy = remote(
                outgoing.at[d - 1, span],
                incoming.at[d - 1, span],
                block_send.at[g, d - 1],
                block_recv.at[g, d - 1],
                device,
            )
            copy.start()
            copies.append(copy)
    for slot in range(slots):
        table_ref[slot] = pick(0, slot)
    place_columns(anchor_col, hit_ref)
    sums_ref[2] = splat(weight_ref, hit_ref, None)
    near_copies[2].start()
    for load in loads[6:]:
        load.wait()
    first, middle, last = slice(0, rim), slice(rim, lines - rim), slice(lines - rim, lines)
    for g, group in enumerate(slot_groups):
        span = slice(group.start, group.stop)
        total = table_ref[span]
        for d in range(count_az - 1):
            copies[g * (count_az - 1) + d].wait()
            total = total + incoming[d, span]
        table_ref[span] = total
        rows = range(group.start * block[0], group.stop * block[0])
        spread_rows(table_ref, wide_ref, rows)
        look_up(
            wide_ref, heights_ref, lane_ref, row_ref, (first, last), rows, g == 0, (0, 0, samples // LANES)
        )
    for part in (first, last):
        flatten_lines(image_ref, factor_ref, heights_ref, flat_ref, part, slice(None))
    beside = pl.ds(pl.multiple_of((1 - rg) * (samples - LANES), LANES), LANES)
    first_ds, last_ds = pl.ds(0, rim), pl.ds(lines - rim, rim)
    above, below = az - 1, az + 1
    up = [
        remote(flat_ref.at[:, first_ds, :], bottom, send.at[1], recv.at[2], {"az": above, "rg": rg}),
        remote(
            flat_ref.at[:, first_ds, beside], bottom_side, send.at[2], recv.at[4], {"az": above, "rg": 1 - rg}
        ),
    ]
    down = [
        remote(flat_ref.at[:, last_ds, :], top, send.at[3], recv.at[1], {"az": below, "rg": rg}),
        remote(
            flat_ref.at[:, last_ds, beside], top_side, send.at[4], recv.at[3], {"az": below, "rg": 1 - rg}
        ),
    ]

    @pl.when(az > 0)
    def _():
        for copy in up:
            copy.start()

    @pl.when(az < count_az - 1)
    def _():
        for copy in down:
            copy.start()

    def middle_part(start_at, stop_at):
        look_up(
            wide_ref,
            heights_ref,
            lane_ref,
            row_ref,
            (middle,),
            range(slots * block[0]),
            True,
            ((1 - rg) * (samples // LANES - 1), start_at, stop_at),
            lambda span: flatten_lines(image_ref, factor_ref, heights_ref, flat_ref, middle, span),
        )

    middle_part(0, 1)
    side_copy = remote(flat_ref.at[:, :, beside], side, send.at[0], recv.at[0], partner)
    side_copy.start()
    middle_part(1, samples // LANES)

    def place(target, centre, nearby):
        left = jnp.where(rg == 1, nearby, 0.0)
        right = jnp.where(rg == 0, nearby, 0.0)
        for part in range(2):
            wide = jnp.concatenate([left[part], centre[part], right[part]], axis=1)
            padded_ref[part, target, :] = wide[:, LANES - rim : 2 * LANES - rim + samples]

    side_copy.wait()
    place(slice(rim, rim + lines), flat_ref[...], side[...])

    @pl.when(az > 0)
    def _():
        for copy in up:
            copy.wait_send()

    @pl.when(az < count_az - 1)
    def _():
        for copy in down:
            copy.wait_send()

    @pl.when(az > 0)
    def _():
        for copy in down:
            copy.wait_recv()
        place(slice(0, rim), top[...], top_side[...])

    @pl.when(az == 0)
    def _():
        padded_ref[:, :rim, :] = jnp.zeros((2, rim, padded_ref.shape[2]), F32)

    @pl.when(az < count_az - 1)
    def _():
        for copy in up:
            copy.wait_recv()
        place(slice(rim + lines, 2 * rim + lines), bottom[...], bottom_side[...])

    @pl.when(az == count_az - 1)
    def _():
        padded_ref[:, rim + lines :, :] = jnp.zeros((2, rim, padded_ref.shape[2]), F32)

    spread(2)
    looks = goldstein_looks(padded_ref, tables)
    sums_ref[0] = splat(weight_ref, hit_ref, looks[0])
    near_copies[0].start()
    sums_ref[1] = splat(weight_ref, hit_ref, looks[1])
    near_copies[1].start()
    spread(0)
    spread(1)
    weight = jnp.maximum(gathered(2), 1.0)
    out_ref[0] = gathered(0) / weight
    out_ref[1] = gathered(1) / weight


def body(
    complex_phase_image,
    phase_to_topography_factor,
    terrain_model_heights,
    radar_parcel_listing,
    pixel_terrain_position,
    multilook_receiving_patch,
    multilook_base_point,
    multilook_splat_shares,
):
    count_az = lax.axis_size("az")
    count_rg = lax.axis_size("rg")
    assert count_rg == 2
    north, east, points = terrain_model_heights.shape
    slots = radar_parcel_listing.shape[1]
    az_lines, rg_samples = phase_to_topography_factor.shape
    dma = pltpu.SemaphoreType.DMA
    block = (points // LANES, LANES)
    rim = PATCH // 4
    cuts = sorted({0, 4 * slots // 9, 7 * slots // 9, slots})
    groups = [range(start, stop) for start, stop in zip(cuts, cuts[1:])]
    tile = (az_lines, rg_samples)
    map_lat = az_lines // LOOK
    map_lon = rg_samples // LOOK
    chunks = map_lat * map_lon // LANES
    whole_lat, whole_lon = map_lat * count_az, map_lon * count_rg
    operands = [
        radar_parcel_listing,
        terrain_model_heights,
        pixel_terrain_position,
        multilook_receiving_patch.reshape(chunks, LANES),
        multilook_base_point.reshape(chunks, LANES),
        multilook_splat_shares,
        phase_to_topography_factor,
        complex_phase_image,
    ] + [jnp.asarray(table) for table in filter_tables()]
    assert len(operands) == 18
    return pl.pallas_call(
        functools.partial(whole_kernel, count_az, rim, groups),
        out_shape=pltpu.VMEM((2, map_lat, map_lon), F32),
        in_specs=[pl.BlockSpec(memory_space=pl.ANY)] * len(operands),
        scratch_shapes=[pltpu.VMEM(x.shape, x.dtype) for x in operands]
        + [
            dma((len(operands),)),
            pltpu.VMEM((north * east + north + 1,) + block, F32),
            pltpu.VMEM((north,) + block, F32),
            pltpu.VMEM((8, LANES), jnp.int32),
            pltpu.VMEM((count_az, 8, LANES), jnp.int32),
            pltpu.SMEM((count_az, 8, LANES), jnp.int32),
            pltpu.VMEM((count_az - 1, slots) + block, F32),
            pltpu.VMEM((count_az - 1, slots) + block, F32),
            pltpu.VMEM((slots,) + block, F32),
            pltpu.VMEM((slots * block[0], 8, LANES), F32),
            pltpu.VMEM(tile, F32),
            pltpu.VMEM(tile, jnp.int32),
            pltpu.VMEM(tile, jnp.int32),
            pltpu.VMEM((2,) + tile, F32),
            pltpu.VMEM((2, rim, rg_samples), F32),
            pltpu.VMEM((2, rim, rg_samples), F32),
            pltpu.VMEM((2, az_lines, LANES), F32),
            pltpu.VMEM((2, rim, LANES), F32),
            pltpu.VMEM((2, rim, LANES), F32),
            dma((2,)),
            dma((count_az - 1,)),
            dma((count_az - 1,)),
            dma((len(groups), count_az - 1)),
            dma((len(groups), count_az - 1)),
            dma,
            dma((5,)),
            dma((5,)),
            pltpu.VMEM((2, az_lines + 2 * rim, rg_samples + LANES), F32),
            pltpu.VMEM((2, whole_lat, chunks * LANES), F32),
            pltpu.VMEM((chunks * LANES, whole_lon), BF16),
            pltpu.VMEM((3, whole_lat, whole_lon), F32),
            pltpu.VMEM((3, whole_lat, map_lon), F32),
            pltpu.VMEM((3, whole_lat, map_lon), F32),
            pltpu.VMEM((3, count_az - 1, map_lat, map_lon), F32),
            dma((3,)),
            dma((3,)),
            dma((3, count_az - 1)),
            dma((3, count_az - 1)),
        ],
        compiler_params=pltpu.CompilerParams(
            collective_id=0, has_side_effects=True, vmem_limit_bytes=56 * 1024 * 1024
        ),
        name="interferogram_map",
    )(*operands)


def solution(mesh):
    return jax.shard_map(
        body,
        mesh=mesh,
        in_specs=(
            P(None, ("scene", "az"), "rg"),
            P(("scene", "az"), "rg"),
            P(("scene", "az"), "rg", None),
            P(("scene", "az", "rg"), None),
            P(("scene", "az"), "rg"),
            P(("scene", "az", "rg"), None),
            P(("scene", "az", "rg")),
            P(None, ("scene", "az", "rg")),
        ),
        out_specs=P(None, ("scene", "az"), "rg"),
        check_vma=False,
    )
```

```python
import functools
import math

import jax
import jax.numpy as jnp
import numpy as np
from jax import lax
from jax.experimental import pallas as pl
from jax.experimental.pallas import tpu as pltpu
from jax.sharding import PartitionSpec as P

PATCH = 64
LOOK = 4
LANES = 128
EPS = 1e-06
F32 = jnp.float32
BF16 = jnp.bfloat16


def halves(value):
    high = value.astype(BF16)
    return high, (value - high.astype(F32)).astype(BF16)


def filter_tables():
    steps = np.arange(PATCH)
    angle = (steps[:, None] * steps[None, :] % PATCH) * (2.0 * math.pi / PATCH)
    cosine, sine = np.cos(angle), np.sin(angle)
    left = np.block([[cosine, sine], [-sine, cosine]])
    step, wide = PATCH // 2, 4 * PATCH
    right = np.zeros((2 * wide, 2 * wide))
    for p in range(4):
        rows, cols = slice(p * step, p * step + PATCH), slice(p * PATCH, (p + 1) * PATCH)
        rows_im = slice(wide + p * step, wide + p * step + PATCH)
        cols_im = slice(wide + p * PATCH, wide + (p + 1) * PATCH)
        right[rows, cols] = cosine
        right[rows, cols_im] = -sine
        right[rows_im, cols] = sine
        right[rows_im, cols_im] = cosine
    group = np.arange(wide) // PATCH
    same = group[:, None] == group[None, :]
    gap = (np.arange(wide)[:, None] - np.arange(wide)[None, :]) % PATCH
    band = same & ((gap <= 1) | (gap == PATCH - 1))
    cells = PATCH // 2 // LOOK
    places = PATCH // 4 + np.arange(cells * LOOK)
    turn = steps[:, None] * places[None, :] % PATCH * (2.0 * math.pi / PATCH)
    mean_re = np.cos(turn).reshape(PATCH, cells, LOOK).mean(axis=2) / PATCH
    mean_im = np.sin(turn).reshape(PATCH, cells, LOOK).mean(axis=2) / PATCH
    back_left = np.block([[mean_re.T, -mean_im.T], [mean_im.T, mean_re.T]])
    back_right = np.zeros((2 * wide, 8 * cells))
    for p in range(4):
        rows = slice(p * PATCH, (p + 1) * PATCH)
        rows_im = slice(wide + p * PATCH, wide + (p + 1) * PATCH)
        cols = slice(p * cells, (p + 1) * cells)
        cols_im = slice((4 + p) * cells, (5 + p) * cells)
        back_right[rows, cols] = mean_re
        back_right[rows, cols_im] = mean_im
        back_right[rows_im, cols] = -mean_im
        back_right[rows_im, cols_im] = mean_re
    tables = []
    for table in (left, right, back_left, back_right):
        high = table.astype(np.float32).astype(jnp.bfloat16)
        tables += [high, (table - high.astype(np.float64)).astype(jnp.bfloat16)]
    return tables + [band.astype(jnp.bfloat16), same.astype(jnp.bfloat16)]


def sine_cosine(angle):
    turns = jnp.floor(angle * (2.0 / math.pi) + 0.5)
    rest = angle - turns * 1.5703125
    rest = rest - turns * 4.837512969970703e-04
    rest = rest - turns * 7.549789948768648e-08
    square = rest * rest
    sine = ((-1.9515295891e-4 * square + 8.3321608736e-3) * square - 1.6666654611e-1) * square
    sine = sine * rest + rest
    cosine = ((2.443315711809948e-5 * square - 1.388731625493765e-3) * square + 4.166664568298827e-2)
    cosine = cosine * square * square - 0.5 * square + 1.0
    quarter = turns.astype(jnp.int32) & 3
    swap = (quarter & 1) == 1
    sine_out = jnp.where(swap, cosine, sine)
    cosine_out = jnp.where(swap, sine, cosine)
    sine_out = jnp.where(quarter >= 2, -sine_out, sine_out)
    cosine_out = jnp.where((quarter == 1) | (quarter == 2), -cosine_out, cosine_out)
    return sine_out, cosine_out


def stacked(left, right):
    rows = left.shape[0]
    high, low = halves(left)
    both = jnp.dot(jnp.concatenate([high, low], axis=0), right[0], preferred_element_type=F32)
    out = both[:rows] + both[rows:]
    if right[1] is None:
        return out
    return out + jnp.dot(high, right[1], preferred_element_type=F32)


def goldstein_looks(padded, tables):
    left_both = jnp.concatenate([tables[0][...], tables[1][...]], axis=0)
    back_both = jnp.concatenate([tables[4][...], tables[5][...]], axis=0)
    right = (tables[2], tables[3])
    back_right = (tables[6], tables[7])
    band, same = tables[8][...], tables[9][...]
    step, wide = PATCH // 2, 4 * PATCH
    lines, samples = padded.shape[1:]
    block_rows = (lines - step) // step
    groups = (samples - LANES) // LANES

    def table_first(both, value):
        rows = both.shape[0] // 2
        high, low = halves(value)
        first = jnp.dot(both, high, preferred_element_type=F32)
        return first[:rows] + first[rows:] + jnp.dot(both[:rows], low, preferred_element_type=F32)

    columns = []
    for u in range(block_rows):
        strip = jnp.concatenate(
            [padded[0, u * step : u * step + PATCH], padded[1, u * step : u * step + PATCH]], axis=0
        )
        columns.append(table_first(left_both, strip))
    windows = [slice(q * LANES, q * LANES + wide) for q in range(groups)]
    real = jnp.concatenate([c[:PATCH, w] for w in windows for c in columns], axis=0)
    imag = jnp.concatenate([c[PATCH:, w] for w in windows for c in columns], axis=0)
    spectrum = stacked(real, (right[0][:wide], right[1][:wide])) + stacked(
        imag, (right[0][wide:], right[1][wide:])
    )
    spec_re, spec_im = spectrum[:, :wide], spectrum[:, wide:]
    size = jnp.sqrt(spec_re * spec_re + spec_im * spec_im)
    across = stacked(size, (band, None))
    patches = groups * block_rows
    pieces = [slice(p * PATCH, (p + 1) * PATCH) for p in range(patches)]
    column_sums = jnp.concatenate(
        [jnp.sum(size[p], axis=0, keepdims=True) for p in pieces], axis=0
    )
    if patches % 16:
        column_sums = jnp.concatenate(
            [column_sums, jnp.zeros((16 - patches % 16, wide), F32)], axis=0
        )
    total = stacked(column_sums, (same, None))
    scale = (1.0 / 9.0) / (total * (1.0 / PATCH**2) + EPS)
    gains = []
    for p, piece in enumerate(pieces):
        part = across[piece]
        around = part + pltpu.roll(part, 1, 0) + pltpu.roll(part, PATCH - 1, 0)
        gains.append(jnp.sqrt(around * scale[p : p + 1]))
    gain = jnp.concatenate(gains, axis=0)
    rows = stacked(spec_re * gain, (back_right[0][:wide], back_right[1][:wide])) + stacked(
        spec_im * gain, (back_right[0][wide:], back_right[1][wide:])
    )
    half = rows.shape[1] // 2
    looks = []
    for u in range(block_rows):
        parts = [rows[pieces[q * block_rows + u]] for q in range(groups)]
        value = jnp.concatenate(
            [
                jnp.concatenate([x[:, :half] for x in parts], axis=1),
                jnp.concatenate([x[:, half:] for x in parts], axis=1),
            ],
            axis=0,
        )
        looks.append(table_first(back_both, value))
    half = looks[0].shape[0] // 2
    return [jnp.concatenate([x[:half] for x in looks], axis=0), jnp.concatenate([x[half:] for x in looks], axis=0)]


def anchors(owner, base, tile_lat, tile_lon, count_rg):
    row = owner // count_rg * tile_lat + base // tile_lon
    return row, owner % count_rg * tile_lon + base % tile_lon


def place_rows(anchor_row, share_ref, row_ref):
    row_ids = lax.broadcasted_iota(jnp.int32, (row_ref.shape[1], LANES), 0)
    for i in range(anchor_row.shape[0]):
        span = slice(i * LANES, (i + 1) * LANES)
        gap = row_ids - anchor_row[i : i + 1]
        for c in range(2):
            upper, lower = share_ref[c : c + 1, span], share_ref[2 + c : 3 + c, span]
            row_ref[c, :, span] = jnp.where(gap == 0, upper, jnp.where(gap == 1, lower, 0.0))


def place_columns(anchor_col, hit_ref):
    col_ids = lax.broadcasted_iota(jnp.int32, (LANES, hit_ref.shape[1]), 1).astype(F32)
    for i in range(anchor_col.shape[0]):
        column = jnp.broadcast_to(anchor_col[i : i + 1].astype(F32), (LANES, LANES)).T
        column = jnp.concatenate([column] * (hit_ref.shape[1] // LANES), axis=1)
        hit_ref[i * LANES : (i + 1) * LANES, :] = jnp.where(column == col_ids, 1.0, 0.0).astype(BF16)


def splat(row_ref, hit_ref, look):
    chunks = hit_ref.shape[0] // LANES
    rows = row_ref.shape[1]
    values = []
    for c in range(2):
        if look is None:
            value = row_ref[c]
        else:
            value = jnp.concatenate(
                [row_ref[c, :, i * LANES : (i + 1) * LANES] * look[i : i + 1] for i in range(chunks)],
                axis=1,
            )
        values += halves(value)
    sums = jnp.dot(jnp.concatenate(values, axis=0), hit_ref[...], preferred_element_type=F32)
    moved = pltpu.roll(sums[2 * rows : 3 * rows] + sums[3 * rows :], 1, 1)
    first = lax.broadcasted_iota(jnp.int32, moved.shape, 1) == 0
    return sums[:rows] + sums[rows : 2 * rows] + jnp.where(first, 0.0, moved)


MESH = pl.DeviceIdType.MESH


def peers(count_az):
    az, rg = lax.axis_index("az"), lax.axis_index("rg")
    others = [{"az": lax.rem(az + d, count_az), "rg": rg} for d in range(1, count_az)]
    return az, rg, others, {"az": az, "rg": 1 - rg}


def greet(devices):
    barrier = pltpu.get_barrier_semaphore()
    for device in devices:
        pl.semaphore_signal(barrier, inc=1, device_id=device, device_id_type=MESH)
    pl.semaphore_wait(barrier, len(devices))


def remote(source, target, send_sem, recv_sem, device):
    return pltpu.make_async_remote_copy(
        src_ref=source,
        dst_ref=target,
        send_sem=send_sem,
        recv_sem=recv_sem,
        device_id=device,
        device_id_type=MESH,
    )


def spread_rows(table_ref, wide_ref, rows):
    for r in rows:
        wide_ref[r] = jnp.broadcast_to(table_ref[r // 8, r % 8 : r % 8 + 1, :], wide_ref.shape[1:])


def look_up(wide_ref, heights_ref, lane_ref, row_ref, pieces, rows, fresh, columns, after=None):
    first, start_at, stop_at = columns
    count_columns = heights_ref.shape[1] // LANES

    def one_column(step, carry):
        column = lax.rem(first + step, count_columns)
        span = pl.ds(pl.multiple_of(column * LANES, LANES), LANES)
        lane = jnp.concatenate([lane_ref[piece, span] for piece in pieces], axis=0)
        row = jnp.concatenate([row_ref[piece, span] for piece in pieces], axis=0)
        if fresh:
            heights = jnp.zeros(lane.shape, F32)
        else:
            heights = jnp.concatenate([heights_ref[piece, span] for piece in pieces], axis=0)
        for r in rows:
            source = jnp.concatenate([wide_ref[r]] * (lane.shape[0] // wide_ref.shape[1]), axis=0)
            picked = jnp.take_along_axis(source, lane, axis=1, mode="promise_in_bounds")
            heights = jnp.where(row == r, picked, heights)
        start = 0
        for piece in pieces:
            count = piece.stop - piece.start
            heights_ref[piece, span] = heights[start : start + count]
            start += count
        if after is not None:
            after(span)
        return carry

    lax.fori_loop(start_at, stop_at, one_column, 0)


def flatten_lines(image_ref, factor_ref, heights_ref, flat_ref, lines, span):
    sine, cosine = sine_cosine(factor_ref[lines, span] * heights_ref[lines, span])
    real, imag = image_ref[0, lines, span], image_ref[1, lines, span]
    flat_ref[0, lines, span] = real * cosine + imag * sine
    flat_ref[1, lines, span] = imag * cosine - real * sine


def whole_kernel(
    count_az,
    rim,
    slot_groups,
    *refs,
):
    sources, refs = refs[:18], refs[18:]
    out_ref, refs = refs[0], refs[1:]
    held, refs = refs[:18], refs[18:]
    list_ref, terrain_ref, position_ref, owner_ref, base_ref, share_ref, factor_ref, image_ref = held[:8]
    tables = held[8:]
    (
        load_sems,
        extended,
        edge,
        own_list,
        lists,
        lists_smem,
        outgoing,
        incoming,
        table_ref,
        wide_ref,
        heights_ref,
        lane_ref,
        row_ref,
        flat_ref,
        top,
        bottom,
        side,
        top_side,
        bottom_side,
        edge_sems,
        list_send,
        list_recv,
        block_send,
        block_recv,
        local_sem,
        send,
        recv,
        padded_ref,
        weight_ref,
        hit_ref,
        sums_ref,
        half,
        near,
        far,
        near_send,
        near_recv,
        far_send,
        far_recv,
    ) = refs
    north, east = terrain_ref.shape[:2]
    slots = list_ref.shape[1]
    block = extended.shape[1:]
    lines, samples = factor_ref.shape
    az, rg, others, partner = peers(count_az)
    barrier = pltpu.get_barrier_semaphore()
    crossed = [
        {"az": lax.rem(az + d, count_az), "rg": 1 - rg} for d in (1, count_az - 1)
    ]
    greeted = others + [partner] + crossed
    loads = [
        pltpu.make_async_copy(source, target, load_sems.at[n])
        for n, (source, target) in enumerate(zip(sources, held))
    ]
    for load in loads[:2]:
        load.start()
    for device in greeted:
        pl.semaphore_signal(barrier, inc=1, device_id=device, device_id_type=MESH)
    for load in loads[2:8]:
        load.start()
    loads[0].wait()
    own_list[...] = jnp.full(own_list.shape, -1, jnp.int32)
    own_list[0:1, 0:slots] = list_ref[...]
    lists[0] = own_list[...]
    pl.semaphore_wait(barrier, len(greeted))
    list_copies = [
        remote(own_list, lists.at[d + 1], list_send.at[d], list_recv.at[d], device)
        for d, device in enumerate(others)
    ]
    for copy in list_copies:
        copy.start()
    loads[1].wait()
    for lat in range(north):
        extended[lat * east : (lat + 1) * east] = terrain_ref[lat].reshape((east,) + block)
    extended[north * east + north] = jnp.zeros(block, F32)
    for lat in range(north):
        edge[lat] = jnp.where(rg == 0, extended[lat * east + east - 1], extended[lat * east])
    edge_copy = remote(
        edge, extended.at[pl.ds(north * east, north)], edge_sems.at[0], edge_sems.at[1], partner
    )
    edge_copy.start()
    for load in loads[8:]:
        load.start()
    channels, map_lat, map_lon = sums_ref.shape
    tile, lanes = out_ref.shape[1:]
    mine = pl.ds(pl.multiple_of(rg * lanes, LANES), lanes)
    theirs = pl.ds(pl.multiple_of((1 - rg) * lanes, LANES), lanes)
    near_copies = [
        remote(sums_ref.at[c, :, theirs], near.at[c], near_send.at[c], near_recv.at[c], partner)
        for c in range(channels)
    ]
    far_copies = [
        [
            remote(
                half.at[c, pl.ds(pl.multiple_of(device["az"] * tile, 8), tile), :],
                far.at[c, d],
                far_send.at[c, d],
                far_recv.at[c, d],
                device,
            )
            for d, device in enumerate(others)
        ]
        for c in range(channels)
    ]

    def spread(c):
        near_copies[c].wait()
        half[c] = sums_ref[c, :, mine] + near[c]
        for copy in far_copies[c]:
            copy.start()

    def gathered(c):
        total = half[c, pl.ds(pl.multiple_of(az * tile, 8), tile), :]
        for d, copy in enumerate(far_copies[c]):
            copy.wait()
            total = total + far[c, d]
        return total

    loads[2].wait()
    position = position_ref[...]
    lane_ref[...] = position & (LANES - 1)
    row_ref[...] = lax.shift_right_logical(position, LANES.bit_length() - 1)
    for n in range(3, 6):
        loads[n].wait()
    anchor_row, anchor_col = anchors(owner_ref[...], base_ref[...], tile, lanes, map_lon // lanes)
    place_rows(anchor_row, share_ref, weight_ref)
    for copy in list_copies:
        copy.wait()
    to_smem = pltpu.make_async_copy(lists, lists_smem, local_sem)
    to_smem.start()
    edge_copy.wait()
    to_smem.wait()

    def pick(d, slot):
        number = lists_smem[d, 0, slot]
        lat = lax.div(number, 2 * east) - az * north
        lon = lax.rem(number, 2 * east) - rg * east
        inside = (number >= 0) & (lat >= 0) & (lat < north)
        at_edge = (lon < 0) | (lon >= east)
        place = jnp.where(at_edge, north * east + lat, lat * east + lon)
        return extended[jnp.where(inside, place, north * east + north)]

    copies = []
    for g, group in enumerate(slot_groups):
        span = pl.ds(group.start, len(group))
        for d in range(1, count_az):
            for slot in group:
                outgoing[d - 1, slot] = pick(d, slot)
            device = {"az": lax.rem(az + count_az - d, count_az), "rg": rg}
            copy = remote(
                outgoing.at[d - 1, span],
                incoming.at[d - 1, span],
                block_send.at[g, d - 1],
                block_recv.at[g, d - 1],
                device,
            )
            copy.start()
            copies.append(copy)
    for slot in range(slots):
        table_ref[slot] = pick(0, slot)
    place_columns(anchor_col, hit_ref)
    sums_ref[2] = splat(weight_ref, hit_ref, None)
    near_copies[2].start()
    for load in loads[6:]:
        load.wait()
    first, middle, last = slice(0, rim), slice(rim, lines - rim), slice(lines - rim, lines)
    for g, group in enumerate(slot_groups):
        span = slice(group.start, group.stop)
        total = table_ref[span]
        for d in range(count_az - 1):
            copies[g * (count_az - 1) + d].wait()
            total = total + incoming[d, span]
        table_ref[span] = total
        rows = range(group.start * block[0], group.stop * block[0])
        spread_rows(table_ref, wide_ref, rows)
        look_up(
            wide_ref, heights_ref, lane_ref, row_ref, (first, last), rows, g == 0, (0, 0, samples // LANES)
        )
    for part in (first, last):
        flatten_lines(image_ref, factor_ref, heights_ref, flat_ref, part, slice(None))
    beside = pl.ds(pl.multiple_of((1 - rg) * (samples - LANES), LANES), LANES)
    first_ds, last_ds = pl.ds(0, rim), pl.ds(lines - rim, rim)
    above, below = az - 1, az + 1
    up = [
        remote(flat_ref.at[:, first_ds, :], bottom, send.at[1], recv.at[2], {"az": above, "rg": rg}),
        remote(
            flat_ref.at[:, first_ds, beside], bottom_side, send.at[2], recv.at[4], {"az": above, "rg": 1 - rg}
        ),
    ]
    down = [
        remote(flat_ref.at[:, last_ds, :], top, send.at[3], recv.at[1], {"az": below, "rg": rg}),
        remote(
            flat_ref.at[:, last_ds, beside], top_side, send.at[4], recv.at[3], {"az": below, "rg": 1 - rg}
        ),
    ]

    @pl.when(az > 0)
    def _():
        for copy in up:
            copy.start()

    @pl.when(az < count_az - 1)
    def _():
        for copy in down:
            copy.start()

    def middle_part(start_at, stop_at):
        look_up(
            wide_ref,
            heights_ref,
            lane_ref,
            row_ref,
            (middle,),
            range(slots * block[0]),
            True,
            ((1 - rg) * (samples // LANES - 1), start_at, stop_at),
            lambda span: flatten_lines(image_ref, factor_ref, heights_ref, flat_ref, middle, span),
        )

    middle_part(0, 1)
    side_copy = remote(flat_ref.at[:, :, beside], side, send.at[0], recv.at[0], partner)
    side_copy.start()
    middle_part(1, samples // LANES)

    spread(2)

    def place(target, centre, nearby):
        left = jnp.where(rg == 1, nearby, 0.0)
        right = jnp.where(rg == 0, nearby, 0.0)
        for part in range(2):
            wide = jnp.concatenate([left[part], centre[part], right[part]], axis=1)
            padded_ref[part, target, :] = wide[:, LANES - rim : 2 * LANES - rim + samples]

    side_copy.wait()
    place(slice(rim, rim + lines), flat_ref[...], side[...])

    @pl.when(az > 0)
    def _():
        for copy in up:
            copy.wait_send()

    @pl.when(az < count_az - 1)
    def _():
        for copy in down:
            copy.wait_send()

    @pl.when(az > 0)
    def _():
        for copy in down:
            copy.wait_recv()
        place(slice(0, rim), top[...], top_side[...])

    @pl.when(az == 0)
    def _():
        padded_ref[:, :rim, :] = jnp.zeros((2, rim, padded_ref.shape[2]), F32)

    @pl.when(az < count_az - 1)
    def _():
        for copy in up:
            copy.wait_recv()
        place(slice(rim + lines, 2 * rim + lines), bottom[...], bottom_side[...])

    @pl.when(az == count_az - 1)
    def _():
        padded_ref[:, rim + lines :, :] = jnp.zeros((2, rim, padded_ref.shape[2]), F32)

    looks = goldstein_looks(padded_ref, tables)
    sums_ref[0] = splat(weight_ref, hit_ref, looks[0])
    near_copies[0].start()
    sums_ref[1] = splat(weight_ref, hit_ref, looks[1])
    near_copies[1].start()
    spread(0)
    spread(1)
    weight = jnp.maximum(gathered(2), 1.0)
    out_ref[0] = gathered(0) / weight
    out_ref[1] = gathered(1) / weight


def body(
    complex_phase_image,
    phase_to_topography_factor,
    terrain_model_heights,
    radar_parcel_listing,
    pixel_terrain_position,
    multilook_receiving_patch,
    multilook_base_point,
    multilook_splat_shares,
):
    count_az = lax.axis_size("az")
    count_rg = lax.axis_size("rg")
    assert count_rg == 2
    north, east, points = terrain_model_heights.shape
    slots = radar_parcel_listing.shape[1]
    az_lines, rg_samples = phase_to_topography_factor.shape
    dma = pltpu.SemaphoreType.DMA
    block = (points // LANES, LANES)
    rim = PATCH // 4
    cuts = sorted({0, 4 * slots // 9, 7 * slots // 9, slots})
    groups = [range(start, stop) for start, stop in zip(cuts, cuts[1:])]
    tile = (az_lines, rg_samples)
    map_lat = az_lines // LOOK
    map_lon = rg_samples // LOOK
    chunks = map_lat * map_lon // LANES
    whole_lat, whole_lon = map_lat * count_az, map_lon * count_rg
    operands = [
        radar_parcel_listing,
        terrain_model_heights,
        pixel_terrain_position,
        multilook_receiving_patch.reshape(chunks, LANES),
        multilook_base_point.reshape(chunks, LANES),
        multilook_splat_shares,
        phase_to_topography_factor,
        complex_phase_image,
    ] + [jnp.asarray(table) for table in filter_tables()]
    assert len(operands) == 18
    return pl.pallas_call(
        functools.partial(whole_kernel, count_az, rim, groups),
        out_shape=pltpu.VMEM((2, map_lat, map_lon), F32),
        in_specs=[pl.BlockSpec(memory_space=pl.ANY)] * len(operands),
        scratch_shapes=[pltpu.VMEM(x.shape, x.dtype) for x in operands]
        + [
            dma((len(operands),)),
            pltpu.VMEM((north * east + north + 1,) + block, F32),
            pltpu.VMEM((north,) + block, F32),
            pltpu.VMEM((8, LANES), jnp.int32),
            pltpu.VMEM((count_az, 8, LANES), jnp.int32),
            pltpu.SMEM((count_az, 8, LANES), jnp.int32),
            pltpu.VMEM((count_az - 1, slots) + block, F32),
            pltpu.VMEM((count_az - 1, slots) + block, F32),
            pltpu.VMEM((slots,) + block, F32),
            pltpu.VMEM((slots * block[0], 8, LANES), F32),
            pltpu.VMEM(tile, F32),
            pltpu.VMEM(tile, jnp.int32),
            pltpu.VMEM(tile, jnp.int32),
            pltpu.VMEM((2,) + tile, F32),
            pltpu.VMEM((2, rim, rg_samples), F32),
            pltpu.VMEM((2, rim, rg_samples), F32),
            pltpu.VMEM((2, az_lines, LANES), F32),
            pltpu.VMEM((2, rim, LANES), F32),
            pltpu.VMEM((2, rim, LANES), F32),
            dma((2,)),
            dma((count_az - 1,)),
            dma((count_az - 1,)),
            dma((len(groups), count_az - 1)),
            dma((len(groups), count_az - 1)),
            dma,
            dma((5,)),
            dma((5,)),
            pltpu.VMEM((2, az_lines + 2 * rim, rg_samples + LANES), F32),
            pltpu.VMEM((2, whole_lat, chunks * LANES), F32),
            pltpu.VMEM((chunks * LANES, whole_lon), BF16),
            pltpu.VMEM((3, whole_lat, whole_lon), F32),
            pltpu.VMEM((3, whole_lat, map_lon), F32),
            pltpu.VMEM((3, whole_lat, map_lon), F32),
            pltpu.VMEM((3, count_az - 1, map_lat, map_lon), F32),
            dma((3,)),
            dma((3,)),
            dma((3, count_az - 1)),
            dma((3, count_az - 1)),
        ],
        compiler_params=pltpu.CompilerParams(
            collective_id=0, has_side_effects=True, vmem_limit_bytes=56 * 1024 * 1024
        ),
        name="interferogram_map",
    )(*operands)


def solution(mesh):
    return jax.shard_map(
        body,
        mesh=mesh,
        in_specs=(
            P(None, ("scene", "az"), "rg"),
            P(("scene", "az"), "rg"),
            P(("scene", "az"), "rg", None),
            P(("scene", "az", "rg"), None),
            P(("scene", "az"), "rg"),
            P(("scene", "az", "rg"), None),
            P(("scene", "az", "rg")),
            P(None, ("scene", "az", "rg")),
        ),
        out_specs=P(None, ("scene", "az"), "rg"),
        check_vma=False,
    )
```
